256 devices in a mesh: gy: 32 (over x, y, core), gz: 8 (over z).
Axes of the slice: x: 4, y: 4, z: 8, core: 2. Of those that a mesh axis runs over, the one named last changes fastest.
Arguments:
- spectrum: bfloat16 [2, 8, 8192, 1536], P(None, 'gz', 'gy'), may hold values from -2000 to 2000
- layer_index: int32 [1536], replicated, may hold values from 0 to 7, as said below
- y_bounds: int32 [33], replicated, may hold values from 0 to 8192, as said below
- z_bounds: int32 [9], replicated, may hold values from 0 to 1536, as said below
- vp: bfloat16 [10240, 15360], P('gy', 'gz'), may hold values from 3 to 6
- vs: bfloat16 [10240, 15360], P('gy', 'gz'), may hold values from 1.5 to 3.5
- rho: bfloat16 [10240, 15360], P('gy', 'gz'), may hold values from 2 to 2.796875
Outputs:
- new_vp: float32 [10240, 15360], P('gy', 'gz')
- new_vs: float32 [10240, 15360], P('gy', 'gz')
- new_rho: float32 [10240, 15360], P('gy', 'gz')
The draws below stay inside these ranges and needn't reach their ends.
Inputs may be any that keep to these rules, and one draw needn't show every extreme that they name: `layer_index`: never falls with depth; the first cell is in layer 0 and the last in layer 7. `y_bounds`: starts at 0 and ends at 8192; each brick row spans from 192 to 320 cells, and in every draw some row spans exactly 320 and some exactly 192. `z_bounds`: starts at 0 and ends at 1536; each brick column spans from 3 * 1536 // (4 * 8) to 240 cells, and in every draw some column spans exactly 240 and some exactly the least.
All inputs are finite; a program needn't handle non-finite values.
Results may differ from the reference program's by a relative error of at most 0.0013.
Values may be sent and summed in bfloat16 or wider, within the bound.
No kernel may reach another device: no remote copies, remote signals or barrier semaphores. Data moves between devices by JAX's collectives and lax.ppermute only.
A program may use at most 128 MiB of HBM per device.

```python
import math
import jax
import jax.numpy as jnp
from jax import lax

NY = 8192
NZ = 1536
LAYERS = 8
X = 8
YCAP = 320
ZCAP = 240
N_GY = 32
N_GZ = 8


def brick_edges(key, pieces, whole):
    average = whole // pieces
    half_count = pieces // 2
    key_shift, key_order = jax.random.split(key)
    shifts = jax.random.randint(key_shift, (half_count,), 0, average // 4 + 1)
    shifts = jnp.where(jnp.arange(half_count) == 0, average // 4, shifts)
    extents = jnp.concatenate([average + shifts, average - shifts])
    extents = extents[jax.random.permutation(key_order, pieces)]
    edges = jnp.concatenate([jnp.zeros((1,), jnp.int32), jnp.cumsum(extents).astype(jnp.int32)])
    return edges.astype(jnp.int32)


def draw_spectrum(key, part):
    key = jax.random.fold_in(key, 11)
    key_values, key_rows, key_cols, key_modes, key_gains = jax.random.split(key, 5)
    mode_scale = 0.034 * math.sqrt(NY * NZ)
    values = jax.random.normal(key_values, (2, X, NY, NZ), jnp.float32)
    log_top = math.log(10.0)
    low_modes = jax.random.normal(key_modes, (2, X, 3, 3), jnp.float32) * mode_scale
    row_scale = jnp.exp(jax.random.uniform(key_rows, (1, 1, NY, 1), jnp.float32, 0.0, log_top))
    col_scale = jnp.exp(jax.random.uniform(key_cols, (1, 1, 1, NZ), jnp.float32, 0.0, log_top))
    rough_part = values * row_scale * col_scale / 16.0
    low_rows = jnp.array([0, 1, NY - 1], dtype=jnp.int32)
    low_cols = jnp.array([0, 1, NZ - 1], dtype=jnp.int32)
    with_modes = rough_part.at[:, :, low_rows[:, None], low_cols[None, :]].set(low_modes)
    gain_range = 0.5 * math.log(10.0)
    plane_gain = jnp.exp(jax.random.uniform(key_gains, (1, X, 1, 1), jnp.float32, -gain_range, gain_range))
    return jnp.clip(with_modes * plane_gain, -2000.0, 2000.0).astype(jnp.bfloat16)


def draw_layer_index(key, part):
    key = jax.random.fold_in(key, 21)
    spacing = NZ // LAYERS
    jitter = jax.random.randint(key, (LAYERS - 1,), -(spacing // 4), spacing // 4 + 1)
    bounds = jnp.arange(1, LAYERS, dtype=jnp.int32) * spacing + jitter
    depths = jnp.arange(NZ, dtype=jnp.int32)
    return jnp.sum((depths[:, None] >= bounds[None, :]).astype(jnp.int32), axis=1).astype(jnp.int32)


def draw_y_bounds(key, part):
    key = jax.random.fold_in(key, 31)
    return brick_edges(key, N_GY, NY)


def draw_z_bounds(key, part):
    key = jax.random.fold_in(key, 41)
    return brick_edges(key, N_GZ, NZ)


def block_levels(stream_key, dims, cuts, low, high):
    def one(axis_at, blocks):
        draws = jax.random.uniform(jax.random.fold_in(jax.random.fold_in(stream_key, 6), axis_at), (blocks,), jnp.float32, low / len(cuts), high / len(cuts))
        return jnp.repeat(jnp.exp(draws), dims[axis_at] // blocks).reshape((-1,) + (1,) * (len(dims) - axis_at - 1))

    loudness = one(*cuts[0])
    for cut in cuts[1:]:
        loudness = loudness * one(*cut)
    return loudness


def setup_inputs(seed: int = 0) -> dict:
    keys = jax.random.split(jax.random.key(seed), 8)
    return {
        "spectrum": draw_spectrum(jax.random.fold_in(keys[7], 71), 0),
        "layer_index": draw_layer_index(jax.random.fold_in(keys[7], 71), 0),
        "y_bounds": draw_y_bounds(jax.random.fold_in(keys[7], 71), 0),
        "z_bounds": draw_z_bounds(jax.random.fold_in(keys[7], 71), 0),
        "vp": jnp.clip(3.0 + 3.0 * jax.random.uniform(keys[4], (N_GY * YCAP, N_GZ * ZCAP * X), jnp.float32) ** block_levels(keys[4], (N_GY * YCAP, N_GZ * ZCAP * X), ((0, 32), (1, 8)), -0.2, 0.2), 3.0, 6.0).astype(jnp.bfloat16),
        "vs": jnp.clip(1.5 + 2.0 * jax.random.uniform(keys[5], (N_GY * YCAP, N_GZ * ZCAP * X), jnp.float32) ** block_levels(keys[5], (N_GY * YCAP, N_GZ * ZCAP * X), ((0, 32), (1, 8)), -0.2, 0.2), 1.5, 3.5).astype(jnp.bfloat16),
        "rho": jnp.clip(2.0 + 0.796875 * jax.random.uniform(keys[6], (N_GY * YCAP, N_GZ * ZCAP * X), jnp.float32) ** block_levels(keys[6], (N_GY * YCAP, N_GZ * ZCAP * X), ((0, 32), (1, 8)), -0.2, 0.2), 2.0, 2.796875).astype(jnp.bfloat16),
    }


CORRELATION = 8.0
HURST_EXPONENT = 0.1
SPREAD_SIGMA = 0.1
DENSITY_GAIN = 0.8
EPSILON = 1e-06

def signed_waves(pieces):
    position = jnp.arange(pieces, dtype=jnp.int32)
    signed = jnp.where(2 * position < pieces, position, position - pieces)
    return signed.astype(jnp.float32) * (2.0 * math.pi / pieces)

def spread(first_axis, second_axis):
    squares = first_axis[:, None] * first_axis[:, None] + second_axis[None, :] * second_axis[None, :]
    return (1.0 + CORRELATION * CORRELATION * squares) ** (-(HURST_EXPONENT + 1.0) / 2.0)

def slot_table(bounds, capacity, limit):
    pieces = bounds.shape[0] - 1
    slot_index = jnp.arange(pieces * capacity, dtype=jnp.int32)
    owners = slot_index // capacity
    offset = slot_index - owners * capacity
    matches = owners[:, None] == jnp.arange(pieces, dtype=jnp.int32)[None, :]
    starts = lax.optimization_barrier(jnp.sum(jnp.where(matches, bounds[None, :pieces], 0), axis=1)).astype(jnp.int32)
    finish = lax.optimization_barrier(jnp.sum(jnp.where(matches, bounds[None, 1:], 0), axis=1)).astype(jnp.int32)
    return (jnp.minimum(starts + offset, limit - 1).astype(jnp.int32), offset < finish - starts)

def reference(spectrum, layer_index, y_bounds, z_bounds, vp, vs, rho):
    amplitude = spread(signed_waves(NY), signed_waves(NZ))

    def one_plane(paired):
        values = paired[0].astype(jnp.float32) * amplitude + 1j * (paired[1].astype(jnp.float32) * amplitude)
        across = jnp.fft.ifft(values, axis=1, norm='ortho')
        return jnp.real(jnp.fft.ifft(across, axis=0, norm='ortho')).astype(jnp.float32)
    field = lax.map(one_plane, jnp.swapaxes(spectrum, 0, 1))
    taper = (layer_index.astype(jnp.float32) + 1.0) / LAYERS
    tapered = field * taper[None, None, :]
    factor = SPREAD_SIGMA / jnp.sqrt(jnp.sum(tapered * tapered) / (X * NY * NZ) + EPSILON)
    perturbation = tapered * factor
    row_index, row_valid = slot_table(y_bounds, YCAP, NY)
    col_index, col_valid = slot_table(z_bounds, ZCAP, NZ)
    picked = jnp.take(jnp.take(perturbation, row_index, axis=1), col_index, axis=2)
    picked = jnp.transpose(picked, (1, 2, 0))
    valid_cells = (row_valid[:, None] & col_valid[None, :])[:, :, None]
    slots_shape = (N_GY * YCAP, N_GZ * ZCAP, X)
    flat_shape = (N_GY * YCAP, N_GZ * ZCAP * X)
    vp_cells = vp.astype(jnp.float32).reshape(slots_shape)
    vs_cells = vs.astype(jnp.float32).reshape(slots_shape)
    rho_cells = rho.astype(jnp.float32).reshape(slots_shape)
    new_vp = jnp.where(valid_cells, vp_cells * (1.0 + picked), 0.0).reshape(flat_shape)
    new_vs = jnp.where(valid_cells, vs_cells * (1.0 + picked), 0.0).reshape(flat_shape)
    new_rho = jnp.where(valid_cells, rho_cells * (1.0 + DENSITY_GAIN * picked), 0.0).reshape(flat_shape)
    return (new_vp, new_vs, new_rho)
```

```python
import functools
import math

import jax
import jax.numpy as jnp
import numpy as np
from jax import lax
from jax.experimental import pallas as pl
from jax.experimental.pallas import tpu as pltpu
from jax.sharding import PartitionSpec as P

LAYERS = 8
CORRELATION = 8.0
HURST_EXPONENT = 0.1
SPREAD_SIGMA = 0.1
DENSITY_GAIN = 0.8
EPSILON = 1e-06

NY, NZ, X = 8192, 1536, 8
GY, GZ = 32, 8
ROWS = NY // GY
BAND = NZ // GY
YCAP, ZCAP = 320, 240
INNER = 128
OUTER = NZ // INNER
RADIX = 8
LONG = NY // RADIX
STEP = YCAP // RADIX
PER = 3
WIDE = 384
SLOT = 256
f32, bf16 = jnp.float32, jnp.bfloat16
MIB = 1024 * 1024


def inner_table():
    angle = 2.0 * np.pi * (np.outer(np.arange(INNER), np.arange(INNER)) % INNER) / INNER
    c, s = np.cos(angle), np.sin(angle)
    return np.block([[c, -s], [s, c]]).astype(bf16)


def depth_twist():
    angle = 2.0 * np.pi * np.outer(np.arange(OUTER), np.arange(INNER)) / NZ
    return np.stack([np.cos(angle), np.sin(angle)], axis=1).reshape(2 * OUTER, INNER).astype(np.float32)


def y_table():
    angle = 2.0 * np.pi * (np.outer(np.arange(LONG), np.arange(LONG)) % LONG) / LONG
    full = np.concatenate([np.cos(angle), -np.sin(angle)], axis=0).astype(bf16)
    return np.ascontiguousarray(full.reshape(2 * LONG, LONG // 256, 256).transpose(1, 0, 2))


def y_twist():
    angle = 2.0 * np.pi * np.outer(np.arange(RADIX), np.arange(LONG)) / NY
    both = np.stack([np.cos(angle), np.sin(angle)], axis=1).astype(np.float32)
    split = both.reshape(2 * RADIX, LONG // ROWS, ROWS).transpose(1, 0, 2)
    return np.ascontiguousarray(split)


def weave_table():
    rows = np.arange(X * 128)
    plane, slot = rows // 128, rows % 128
    full = np.zeros((X * 128, X * 128), np.float32)
    full[rows, slot * X + plane] = 1.0
    return np.ascontiguousarray(full.reshape(X * 128, 4, 256).transpose(1, 0, 2)).astype(bf16)


def four(a):
    (r0, i0), (r1, i1), (r2, i2), (r3, i3) = a
    sr, si, dr, di = r0 + r2, i0 + i2, r0 - r2, i0 - i2
    tr, ti, er, ei = r1 + r3, i1 + i3, r1 - r3, i1 - i3
    return [(sr + tr, si + ti), (dr - ei, di + er), (sr - tr, si - ti), (dr + ei, di - er)]


def three(a):
    (r0, i0), (r1, i1), (r2, i2) = a
    tr, ti = r1 + r2, i1 + i2
    half = math.sqrt(3.0) / 2.0
    er, ei = (r1 - r2) * half, (i1 - i2) * half
    mr, mi = r0 - 0.5 * tr, i0 - 0.5 * ti
    return [(r0 + tr, i0 + ti), (mr - ei, mi + er), (mr + ei, mi - er)]


def twelve(a):
    quarter = [four([a[(4 * i + 3 * j) % 12] for j in range(4)]) for i in range(3)]
    out = [None] * 12
    for v in range(4):
        for u, value in enumerate(three([quarter[i][v] for i in range(3)])):
            out[next(q for q in range(12) if q % 3 == u and q % 4 == v)] = value
    return out


def eight(a):
    even, odd = four(a[0::2]), four(a[1::2])
    h = math.sqrt(0.5)
    (r0, i0), (r1, i1), (r2, i2), (r3, i3) = odd
    turned = [(r0, i0), ((r1 - i1) * h, (r1 + i1) * h), (-i2, r2), ((-r3 - i3) * h, (r3 - i3) * h)]
    first = [(e[0] + t[0], e[1] + t[1]) for e, t in zip(even, turned)]
    last = [(e[0] - t[0], e[1] - t[1]) for e, t in zip(even, turned)]
    return first + last


def depth_kernel(place_ref, spec_ref, twist_ref, table_ref, out_ref, mid_ref, hold_ref):
    first = place_ref[0] * ROWS
    lane = lax.broadcasted_iota(jnp.int32, (16, INNER), 1)
    line = lax.broadcasted_iota(jnp.int32, (16, INNER), 0)

    def rows_at(step, carry):
        at = pl.multiple_of(step * 16, 16)
        ky = first + at + line
        wy = jnp.where(2 * ky < NY, ky, ky - NY).astype(f32) * (2.0 * math.pi / NY)
        wy2 = wy * wy
        values = []
        for p in range(OUTER):
            kz = lane + p * INNER
            wz = jnp.where(2 * kz < NZ, kz, kz - NZ).astype(f32) * (2.0 * math.pi / NZ)
            base = 1.0 + CORRELATION * CORRELATION * (wy2 + wz * wz)
            gain = jnp.exp(jnp.log(base) * (-(HURST_EXPONENT + 1.0) / 2.0)) * (1.0 / math.sqrt(NY * NZ))
            span = pl.ds(p * INNER, INNER)
            values.append(
                (
                    spec_ref[0, pl.ds(at, 16), span].astype(f32) * gain,
                    spec_ref[1, pl.ds(at, 16), span].astype(f32) * gain,
                )
            )
        for q, (re, im) in enumerate(twelve(values)):
            c = twist_ref[pl.ds(2 * q, 1), :]
            s = twist_ref[pl.ds(2 * q + 1, 1), :]
            mid_ref[q, pl.ds(at, 16), pl.ds(0, INNER)] = (re * c - im * s).astype(bf16)
            mid_ref[q, pl.ds(at, 16), pl.ds(INNER, INNER)] = (re * s + im * c).astype(bf16)
        return carry

    lax.fori_loop(0, ROWS // 16, rows_at, 0)
    for q in range(OUTER):
        made = lax.dot_general(
            table_ref[...], mid_ref[q], (((1,), (1,)), ((), ())), preferred_element_type=f32
        )
        for half in range(2):
            for part in range(2):
                hold_ref[half, part, pl.ds(q, INNER, stride=OUTER), :] = made[
                    part * INNER : (part + 1) * INNER, half * 128 : (half + 1) * 128
                ]

    def pack(step, carry):
        at = pl.multiple_of(step * BAND, BAND)
        for part in range(2):
            for half in range(2):
                out_ref[step, pl.ds(part * BAND, BAND), pl.ds(half * 128, 128)] = hold_ref[
                    half, part, pl.ds(at, BAND), :
                ].astype(bf16)
        return carry

    lax.fori_loop(0, GY, pack, 0)


def pieces(value):
    high = value.astype(bf16).astype(f32)
    rest = value - high
    middle = rest.astype(bf16).astype(f32)
    return high, middle, rest - middle


def y_kernel(bounds_ref, in_ref, taper_ref, twist_ref, table_ref, out_ref, mid_ref, field_ref):
    groups = LONG // ROWS

    def turn(low, carry):
        for row in range(0, BAND, 16):
            for col in range(0, ROWS, 128):
                values = []
                for e in range(RADIX):
                    block = groups * e + low
                    values.append(
                        (
                            in_ref[block, pl.ds(row, 16), pl.ds(col, 128)].astype(f32),
                            in_ref[block, pl.ds(BAND + row, 16), pl.ds(col, 128)].astype(f32),
                        )
                    )
                lanes = pl.multiple_of(low * ROWS + col, 128)
                for y1, (re, im) in enumerate(eight(values)):
                    c = twist_ref[low, pl.ds(2 * y1, 1), pl.ds(col, 128)]
                    s = twist_ref[low, pl.ds(2 * y1 + 1, 1), pl.ds(col, 128)]
                    at = pl.ds(y1 * BAND + row, 16)
                    mid_ref[at, pl.ds(lanes, 128)] = (re * c - im * s).astype(bf16)
                    mid_ref[at, pl.ds(pl.multiple_of(lanes + LONG, 128), 128)] = (re * s + im * c).astype(bf16)
        return carry

    lax.fori_loop(0, groups, turn, 0)
    total = jnp.zeros((8, 128), f32)
    taper = taper_ref[...]
    for block in range(LONG // 256):
        made = jnp.dot(mid_ref[...], table_ref[block], preferred_element_type=f32)
        for half in range(2):
            part = made[:, half * 128 : (half + 1) * 128] * taper
            field_ref[2 * block + half] = part
            total = total + jnp.sum((part * part).reshape(RADIX * BAND // 8, 8, 128), axis=0)
    field_ref[LONG // 128] = jnp.zeros((RADIX * BAND, 128), f32)
    sums = jnp.sum(jnp.sum(total, axis=0, keepdims=True), axis=1, keepdims=True)
    high, middle, low = pieces(jnp.broadcast_to(sums, (BAND, 128)))
    lane = lax.broadcasted_iota(jnp.int32, (BAND, 128), 1)
    extra = jnp.where(lane == 125, high, jnp.where(lane == 126, middle, jnp.where(lane == 127, low, 0.0)))

    def window(g, carry):
        start = bounds_ref[g]
        y1_first = lax.rem(start, RADIX)
        y2_first = lax.div(start, RADIX)
        for tile in range(WIDE // 128):
            parts = []
            for y1 in range(tile * PER, min(tile * PER + PER, RADIX)):
                at = y2_first + jnp.where(y1 < y1_first, 1, 0)
                block = lax.div(at, 128)
                shift = lax.rem(at, 128)
                rows = pl.ds(y1 * BAND, BAND)
                both = jnp.where(lane >= shift, field_ref[block, rows, :], field_ref[block + 1, rows, :])
                to = (y1 % PER) * STEP
                parts.append(pltpu.roll(both, lax.rem(to - shift + 128, 128), 1))
            if len(parts) < PER:
                parts.append(extra)
            whole = jnp.where(lane < STEP, parts[0], jnp.where(lane < 2 * STEP, parts[1], parts[2]))
            out_ref[g, :, pl.ds(tile * 128, 128)] = whole.astype(bf16)
        return carry

    lax.fori_loop(0, GY, window, 0)


def brick_kernel(start_ref, bounds_ref, in_ref, out_ref, rows_ref):
    def spread_out(g, carry):
        for tile in range(WIDE // 128):
            part = in_ref[g, :, pl.ds(tile * 128, 128)].astype(f32)
            rows_ref[tile, pl.ds(pl.multiple_of(g * BAND, BAND), BAND), :] = part
        return carry

    lax.fori_loop(0, GY, spread_out, 0)
    rows_ref[:, pl.ds(NZ, SLOT), :] = jnp.zeros((WIDE // 128, SLOT, 128), f32)
    tail = jnp.zeros((16, 128), f32)
    for g in range(GY):
        tail = tail + in_ref[g, pl.ds(0, 16), pl.ds(WIDE - 128, 128)].astype(f32)
    lane16 = lax.broadcasted_iota(jnp.int32, (16, 128), 1)
    sums = jnp.sum(jnp.where(lane16 >= 125, tail, 0.0), axis=1, keepdims=True)[0:1, :]
    high, middle, low = pieces(jnp.broadcast_to(sums, (YCAP, SLOT)))
    lane = lax.broadcasted_iota(jnp.int32, (YCAP, SLOT), 1)
    y1_first = lax.rem(start_ref[0], RADIX)
    r = lax.broadcasted_iota(jnp.int32, (YCAP, WIDE), 0)
    col = lax.broadcasted_iota(jnp.int32, (YCAP, WIDE), 1)
    y1 = (r + y1_first) & (RADIX - 1)
    third = jnp.where(y1 >= 2 * PER, 2, jnp.where(y1 >= PER, 1, 0))
    wanted = third * 128 + (y1 - PER * third) * STEP + (r >> 3)
    choose = jnp.where(col == wanted, 1.0, 0.0).astype(bf16)
    for j in range(GZ):
        at = pl.ds(bounds_ref[j], SLOT)
        picked = jnp.concatenate([rows_ref[tile, at, :] for tile in range(WIDE // 128)], axis=1).astype(bf16)
        made = lax.dot_general(choose, picked, (((1,), (1,)), ((), ())), preferred_element_type=f32)
        made = jnp.where(lane == SLOT - 3, high, made)
        made = jnp.where(lane == SLOT - 2, middle, made)
        made = jnp.where(lane == SLOT - 1, low, made)
        out_ref[j] = made.astype(bf16)


def model_kernel(
    extent_ref, in_ref, weave_ref, vp_ref, vs_ref, rho_ref, new_vp_ref, new_vs_ref, new_rho_ref, factor_ref
):
    step = pl.program_id(0)

    @pl.when(step == 0)
    def _():
        tail = jnp.zeros((16, 128), f32)
        for x in range(X):
            tail = tail + in_ref[x, pl.ds(0, 16), pl.ds(SLOT - 128, 128)].astype(f32)
        lane16 = lax.broadcasted_iota(jnp.int32, (16, 128), 1)
        sums = jnp.sum(jnp.where(lane16 >= 125, tail, 0.0), axis=1, keepdims=True)[0:1, :]
        spread = jnp.broadcast_to(sums, (8, 128))
        factor_ref[...] = SPREAD_SIGMA / jnp.sqrt(spread / (X * NY * NZ) + EPSILON)

    lanes = pl.multiple_of(lax.div(step, 4) * 128, 128)
    planes = jnp.concatenate([in_ref[x, :, pl.ds(lanes, 128)] for x in range(X)], axis=1)
    made = jnp.dot(planes, weave_ref[lax.rem(step, 4)], preferred_element_type=f32)
    row = lax.broadcasted_iota(jnp.int32, (YCAP, 256), 0)
    slot = (lax.broadcasted_iota(jnp.int32, (YCAP, 256), 1) + step * 256) >> 3
    valid = (row < extent_ref[0]) & (slot < extent_ref[1])
    picked = made * factor_ref[0:1, 0:1]
    new_vp_ref[...] = jnp.where(valid, vp_ref[...].astype(f32) * (1.0 + picked), 0.0)
    new_vs_ref[...] = jnp.where(valid, vs_ref[...].astype(f32) * (1.0 + picked), 0.0)
    new_rho_ref[...] = jnp.where(valid, rho_ref[...].astype(f32) * (1.0 + DENSITY_GAIN * picked), 0.0)


SMEM = pl.BlockSpec(memory_space=pltpu.SMEM)
VMEM = pl.BlockSpec(memory_space=pltpu.VMEM)


def depth_stage(place, spec):
    return pl.pallas_call(
        depth_kernel,
        out_shape=jax.ShapeDtypeStruct((GY, 2 * BAND, ROWS), bf16),
        in_specs=[SMEM, VMEM, VMEM, VMEM],
        out_specs=VMEM,
        scratch_shapes=[
            pltpu.VMEM((OUTER, ROWS, 2 * INNER), bf16),
            pltpu.VMEM((2, 2, NZ, 128), f32),
        ],
        compiler_params=pltpu.CompilerParams(vmem_limit_bytes=24 * MIB),
    )(place, spec, depth_twist(), inner_table())


def y_stage(y_bounds, turned, taper):
    return pl.pallas_call(
        y_kernel,
        out_shape=jax.ShapeDtypeStruct((GY, BAND, WIDE), bf16),
        in_specs=[SMEM, VMEM, VMEM, VMEM, VMEM],
        out_specs=VMEM,
        scratch_shapes=[
            pltpu.VMEM((RADIX * BAND, 2 * LONG), bf16),
            pltpu.VMEM((LONG // 128 + 1, RADIX * BAND, 128), f32),
        ],
        compiler_params=pltpu.CompilerParams(vmem_limit_bytes=32 * MIB),
    )(y_bounds, turned, taper, y_twist(), y_table())


def brick_stage(start, z_bounds, windows):
    return pl.pallas_call(
        brick_kernel,
        out_shape=jax.ShapeDtypeStruct((GZ, YCAP, SLOT), bf16),
        in_specs=[SMEM, SMEM, VMEM],
        out_specs=VMEM,
        scratch_shapes=[pltpu.VMEM((WIDE // 128, NZ + SLOT, 128), f32)],
        compiler_params=pltpu.CompilerParams(vmem_limit_bytes=24 * MIB),
    )(start, z_bounds, windows)


def model_stage(extent, bricks, vp, vs, rho):
    flat = X * ZCAP
    wide = pl.BlockSpec((YCAP, 256), lambda i: (0, i))
    return pl.pallas_call(
        model_kernel,
        grid=(-(-flat // 256),),
        out_shape=[jax.ShapeDtypeStruct((YCAP, flat), f32)] * 3,
        in_specs=[
            SMEM,
            pl.BlockSpec((GZ, YCAP, SLOT), lambda i: (0, 0, 0)),
            pl.BlockSpec((4, X * 128, 256), lambda i: (0, 0, 0)),
            wide,
            wide,
            wide,
        ],
        out_specs=[wide] * 3,
        scratch_shapes=[pltpu.VMEM((8, 128), f32)],
        compiler_params=pltpu.CompilerParams(vmem_limit_bytes=32 * MIB),
    )(extent, bricks, weave_table(), vp, vs, rho)


def shards(spectrum, layer_index, y_bounds, z_bounds, vp, vs, rho):
    gy_index = lax.axis_index("gy")
    gz_index = lax.axis_index("gz")
    taper_all = (layer_index.astype(f32) + 1.0) / LAYERS
    taper_band = lax.dynamic_slice_in_dim(taper_all, gy_index * BAND, BAND)
    taper = jnp.broadcast_to(jnp.tile(taper_band, RADIX)[:, None], (RADIX * BAND, 128))
    y_pair = lax.dynamic_slice_in_dim(y_bounds, gy_index, 2)
    z_pair = lax.dynamic_slice_in_dim(z_bounds, gz_index, 2)
    extent = jnp.stack([y_pair[1] - y_pair[0], z_pair[1] - z_pair[0]])

    turned = depth_stage(gy_index.reshape(1), spectrum.reshape(2, ROWS, NZ))
    turned = lax.all_to_all(turned, "gy", 0, 0, tiled=True)
    windows = y_stage(y_bounds, turned, taper)
    windows = lax.all_to_all(windows, "gy", 0, 0, tiled=True)
    bricks = brick_stage(y_pair, z_bounds, windows)
    bricks = lax.all_to_all(bricks, "gz", 0, 0, tiled=True)
    return tuple(model_stage(extent, bricks, vp, vs, rho))


def solution(mesh):
    return jax.shard_map(
        shards,
        mesh=mesh,
        in_specs=(
            P(None, "gz", "gy", None),
            P(),
            P(),
            P(),
            P("gy", "gz"),
            P("gy", "gz"),
            P("gy", "gz"),
        ),
        out_specs=(P("gy", "gz"), P("gy", "gz"), P("gy", "gz")),
        check_vma=False,
    )
```

```python
import functools
import math

import jax
import jax.numpy as jnp
import numpy as np
from jax import lax
from jax.experimental import pallas as pl
from jax.experimental.pallas import tpu as pltpu
from jax.sharding import PartitionSpec as P

LAYERS = 8
CORRELATION = 8.0
HURST_EXPONENT = 0.1
SPREAD_SIGMA = 0.1
DENSITY_GAIN = 0.8
EPSILON = 1e-06

NY, NZ, X = 8192, 1536, 8
GY, GZ = 32, 8
ROWS = NY // GY
CHUNK = 64
BAND = NZ // GY
YCAP, ZCAP = 320, 240
INNER = 128
OUTER = NZ // INNER
RADIX = 8
LONG = NY // RADIX
STEP = YCAP // RADIX + 1
PER = 3
WIDE = 384
MANY = 4
TILES = WIDE // 128
DEEP = 8
PERIOD = GY * DEEP
f32, bf16 = jnp.float32, jnp.bfloat16
MIB = 1024 * 1024


def inner_table():
    angle = 2.0 * np.pi * (np.outer(np.arange(INNER), np.arange(INNER)) % INNER) / INNER
    c, s = np.cos(angle), np.sin(angle)
    return np.block([[c, -s], [s, c]]).astype(bf16)


def depth_twist():
    angle = 2.0 * np.pi * np.outer(np.arange(OUTER), np.arange(INNER)) / NZ
    return np.stack([np.cos(angle), np.sin(angle)], axis=1).reshape(2 * OUTER, INNER).astype(np.float32)


def y_table():
    angle = 2.0 * np.pi * (np.outer(np.arange(LONG), np.arange(LONG)) % LONG) / LONG
    full = np.concatenate([np.cos(angle), -np.sin(angle)], axis=0).astype(bf16)
    return np.ascontiguousarray(full.reshape(2 * LONG, LONG // 256, 256).transpose(1, 0, 2))


def y_twist():
    y1 = np.arange(RADIX)
    angle = 2.0 * np.pi * np.outer(y1 - RADIX * STEP * (y1 % PER), np.arange(LONG)) / NY
    both = np.stack([np.cos(angle), np.sin(angle)], axis=1).astype(np.float32)
    split = both.reshape(2 * RADIX, LONG // ROWS, ROWS).transpose(1, 0, 2)
    return np.ascontiguousarray(split)


def four(a):
    (r0, i0), (r1, i1), (r2, i2), (r3, i3) = a
    sr, si, dr, di = r0 + r2, i0 + i2, r0 - r2, i0 - i2
    tr, ti, er, ei = r1 + r3, i1 + i3, r1 - r3, i1 - i3
    return [(sr + tr, si + ti), (dr - ei, di + er), (sr - tr, si - ti), (dr + ei, di - er)]


def three(a):
    (r0, i0), (r1, i1), (r2, i2) = a
    tr, ti = r1 + r2, i1 + i2
    half = math.sqrt(3.0) / 2.0
    er, ei = (r1 - r2) * half, (i1 - i2) * half
    mr, mi = r0 - 0.5 * tr, i0 - 0.5 * ti
    return [(r0 + tr, i0 + ti), (mr - ei, mi + er), (mr + ei, mi - er)]


def twelve(a):
    quarter = [four([a[(4 * i + 3 * j) % 12] for j in range(4)]) for i in range(3)]
    out = [None] * 12
    for v in range(4):
        for u, value in enumerate(three([quarter[i][v] for i in range(3)])):
            out[next(q for q in range(12) if q % 3 == u and q % 4 == v)] = value
    return out


def eight(a):
    even, odd = four(a[0::2]), four(a[1::2])
    h = math.sqrt(0.5)
    (r0, i0), (r1, i1), (r2, i2), (r3, i3) = odd
    turned = [(r0, i0), ((r1 - i1) * h, (r1 + i1) * h), (-i2, r2), ((-r3 - i3) * h, (r3 - i3) * h)]
    first = [(e[0] + t[0], e[1] + t[1]) for e, t in zip(even, turned)]
    last = [(e[0] - t[0], e[1] - t[1]) for e, t in zip(even, turned)]
    return first + last


def depth_kernel(
    place_ref, spec_ref, twist_hbm_ref, table_hbm_ref, out_ref, rows_ref, mid_ref, hold_ref, twist_ref, table_ref, sem, table_sem
):
    first = place_ref[0] * ROWS
    lane = lax.broadcasted_iota(jnp.int32, (16, INNER), 1)
    line = lax.broadcasted_iota(jnp.int32, (16, INNER), 0)

    def load(k):
        rows = pl.ds(pl.multiple_of(k * CHUNK, CHUNK), CHUNK)
        return pltpu.make_async_copy(spec_ref.at[:, rows, :], rows_ref.at[:, rows, :], sem.at[k])

    fetches = [
        pltpu.make_async_copy(twist_hbm_ref, twist_ref, table_sem.at[0]),
        pltpu.make_async_copy(table_hbm_ref, table_ref, table_sem.at[1]),
    ]
    fetches[0].start()
    for k in range(ROWS // CHUNK):
        load(k).start()
    fetches[1].start()
    fetches[0].wait()

    def rows_at(step, carry):
        at = pl.multiple_of(step * 16, 16)
        ky = first + at + line
        wy = jnp.where(2 * ky < NY, ky, ky - NY).astype(f32) * (2.0 * math.pi / NY)
        wy2 = wy * wy
        values = []
        for p in range(OUTER):
            kz = lane + p * INNER
            wz = jnp.where(2 * kz < NZ, kz, kz - NZ).astype(f32) * (2.0 * math.pi / NZ)
            base = 1.0 + CORRELATION * CORRELATION * (wy2 + wz * wz)
            gain = jnp.exp(jnp.log(base) * (-(HURST_EXPONENT + 1.0) / 2.0)) * (1.0 / math.sqrt(NY * NZ))
            span = pl.ds(p * INNER, INNER)
            values.append(
                (
                    rows_ref[0, pl.ds(at, 16), span].astype(f32) * gain,
                    rows_ref[1, pl.ds(at, 16), span].astype(f32) * gain,
                )
            )
        for q, (re, im) in enumerate(twelve(values)):
            c = twist_ref[pl.ds(2 * q, 1), :]
            s = twist_ref[pl.ds(2 * q + 1, 1), :]
            mid_ref[q, pl.ds(at, 16), pl.ds(0, INNER)] = (re * c - im * s).astype(bf16)
            mid_ref[q, pl.ds(at, 16), pl.ds(INNER, INNER)] = (re * s + im * c).astype(bf16)
        return carry

    def chunk(k, carry):
        load(k).wait()
        lax.fori_loop(k * (CHUNK // 16), (k + 1) * (CHUNK // 16), rows_at, 0)
        return carry

    lax.fori_loop(0, ROWS // CHUNK, chunk, 0)
    fetches[1].wait()
    for q in range(OUTER):
        made = lax.dot_general(
            table_ref[...], mid_ref[q], (((1,), (1,)), ((), ())), preferred_element_type=f32
        )
        for half in range(2):
            for part in range(2):
                hold_ref[half, part, pl.ds(q, INNER, stride=OUTER), :] = made[
                    part * INNER : (part + 1) * INNER, half * 128 : (half + 1) * 128
                ]

    def pack(h, carry):
        for part in range(2):
            for b in range(0, BAND // DEEP, 2):
                for half in range(2):
                    two = [
                        hold_ref[half, part, pl.ds(pl.multiple_of((b + i) * PERIOD + h * DEEP, DEEP), DEEP), :]
                        for i in range(2)
                    ]
                    to = pl.ds(part * BAND + b * DEEP, 2 * DEEP)
                    out_ref[h, to, pl.ds(half * 128, 128)] = jnp.concatenate(two, axis=0).astype(bf16)
        return carry

    lax.fori_loop(0, GY, pack, 0)


def pieces(value):
    high = value.astype(bf16).astype(f32)
    rest = value - high
    middle = rest.astype(bf16).astype(f32)
    return high, middle, rest - middle


def y_kernel(
    place_ref, y_bounds_ref, z_bounds_ref, in_ref, taper_ref, twist_ref, wave_hbm_ref, vp_ref, vs_ref, rho_ref,
    out_ref, vp_out_ref, vs_out_ref, rho_out_ref, mid_ref, field_ref, cut_ref, wave_ref, sem, wave_sem
):
    groups = LONG // ROWS
    models = ((vp_ref, vp_out_ref), (vs_ref, vs_out_ref), (rho_ref, rho_out_ref))
    fetches = [pltpu.make_async_copy(a, b, sem.at[k]) for k, (a, b) in enumerate(models)]
    waves = [pltpu.make_async_copy(wave_hbm_ref.at[k], wave_ref.at[k], wave_sem.at[k]) for k in range(LONG // 256)]
    for fetch in waves + fetches:
        fetch.start()

    def turn(low, carry):
        for row in range(0, BAND, 16):
            for col in range(0, ROWS, 128):
                values = []
                for e in range(RADIX):
                    block = groups * e + low
                    values.append(
                        (
                            in_ref[block, pl.ds(row, 16), pl.ds(col, 128)].astype(f32),
                            in_ref[block, pl.ds(BAND + row, 16), pl.ds(col, 128)].astype(f32),
                        )
                    )
                lanes = pl.multiple_of(low * ROWS + col, 128)
                for y1, (re, im) in enumerate(eight(values)):
                    c = twist_ref[low, pl.ds(2 * y1, 1), pl.ds(col, 128)]
                    s = twist_ref[low, pl.ds(2 * y1 + 1, 1), pl.ds(col, 128)]
                    at = pl.ds(y1 * BAND + row, 16)
                    mid_ref[at, pl.ds(lanes, 128)] = (re * c - im * s).astype(bf16)
                    mid_ref[at, pl.ds(pl.multiple_of(lanes + LONG, 128), 128)] = (re * s + im * c).astype(bf16)
        return carry

    lax.fori_loop(0, groups, turn, 0)
    total = jnp.zeros((8, 128), f32)
    taper = taper_ref[...]
    for block in range(LONG // 256):
        waves[block].wait()
        made = jnp.dot(mid_ref[...], wave_ref[block], preferred_element_type=f32)
        for half in range(2):
            part = made[:, half * 128 : (half + 1) * 128] * taper
            field_ref[2 * block + half] = part
            total = total + jnp.sum((part * part).reshape(RADIX * BAND // 8, 8, 128), axis=0)
    sums = jnp.sum(jnp.sum(total, axis=0, keepdims=True), axis=1, keepdims=True)
    high, middle, low = pieces(jnp.broadcast_to(sums, (BAND, 128)))
    lane = lax.broadcasted_iota(jnp.int32, (BAND, 128), 1)
    extra = jnp.where(lane == 125, high, jnp.where(lane == 126, middle, jnp.where(lane == 127, low, 0.0)))
    for i in range(MANY):
        cut_ref[i, :, pl.ds(BAND, DEEP), :] = jnp.zeros((TILES, DEEP, 128), f32)
        cut_ref[i, TILES - 1, pl.ds(BAND, DEEP), :] = extra[:DEEP]
    here = place_ref[0] * DEEP
    tiles = [lax.div(z_bounds_ref[j] - here + (PERIOD - DEEP), PERIOD) * DEEP for j in range(GZ)]

    def window(g, place):
        y2_first = lax.div(y_bounds_ref[g], RADIX)
        block = lax.div(y2_first, 128)
        later = lax.rem(block + 1, LONG // 128)
        shift = lax.rem(y2_first, 128)
        before = lane < shift
        at = lane - shift + jnp.where(before, 128, 0)
        cut = jnp.minimum(lax.div(127 - shift, STEP), PER - 1)
        split = before & (at < STEP * (cut + 1))
        blocks = [jnp.where(i > cut, later, block) for i in range(PER)]
        for tile in range(TILES):
            parts = []
            for y1 in range(tile * PER, min(tile * PER + PER, RADIX)):
                parts.append(field_ref[blocks[y1 % PER], pl.ds(y1 * BAND, BAND), :])
            whole = jnp.where(at < STEP, parts[0], parts[1])
            if len(parts) == PER:
                whole = jnp.where(at < 2 * STEP, whole, parts[2])
            other = jnp.minimum(tile * PER + cut, RADIX - 1)
            rows = pl.ds(pl.multiple_of(other * BAND, BAND), BAND)
            whole = jnp.where(split, field_ref[later, rows, :], whole)
            whole = pltpu.roll(whole, lax.rem(128 - shift, 128), 1)
            if tile == TILES - 1:
                whole = jnp.where(lane < 2 * STEP, whole, extra)
            cut_ref[place, tile, pl.ds(0, BAND), :] = whole

    def send(g, place):
        for j in range(0, GZ, 2):
            to = pl.ds(pl.multiple_of((g * GZ + j) * DEEP, 2 * DEEP), 2 * DEEP)
            for tile in range(TILES):
                two = [cut_ref[place, tile, pl.ds(pl.multiple_of(tiles[j + i], DEEP), DEEP), :] for i in range(2)]
                out_ref[to, pl.ds(tile * 128, 128)] = jnp.concatenate(two, axis=0).astype(bf16)

    def several(k, carry):
        for i in range(MANY):
            window(k * MANY + i, i)
        for i in range(MANY):
            send(k * MANY + i, i)
        return carry

    lax.fori_loop(0, GY // MANY, several, 0)
    for fetch in fetches:
        fetch.wait()


def model_kernel(
    place_ref, y_bounds_ref, z_bounds_ref, in_ref, vp_ref, vs_ref, rho_ref, new_vp_ref, new_vs_ref, new_rho_ref,
    made_ref, weave_ref, vp_out_ref, vs_out_ref, rho_out_ref, sem
):
    y_first = y_bounds_ref[place_ref[0]]
    y_extent = y_bounds_ref[place_ref[0] + 1] - y_first
    z_first = z_bounds_ref[place_ref[1]]
    z_extent = z_bounds_ref[place_ref[1] + 1] - z_first
    group = X * DEEP
    tail = jnp.zeros((16, 128), f32)
    for k in range(GY * X * DEEP // 16):
        tail = tail + in_ref[pl.ds(16 * k, 16), pl.ds(WIDE - 128, 128)].astype(f32)
    first_row = lax.broadcasted_iota(jnp.int32, (16, 128), 0) % DEEP == 0
    first_row = first_row & (lax.broadcasted_iota(jnp.int32, (16, 128), 1) >= 125)
    total = jnp.sum(jnp.where(first_row, tail, 0.0), axis=0, keepdims=True)
    total = jnp.sum(total, axis=1, keepdims=True)
    factor = SPREAD_SIGMA / jnp.sqrt(total / (X * NY * NZ) + EPSILON)
    r = lax.broadcasted_iota(jnp.int32, (YCAP, WIDE), 0)
    col = lax.broadcasted_iota(jnp.int32, (YCAP, WIDE), 1)
    y = r + lax.rem(y_first, RADIX)
    y1 = y & (RADIX - 1)
    third = jnp.where(y1 >= 2 * PER, 2, jnp.where(y1 >= PER, 1, 0))
    wanted = third * 128 + (y1 - PER * third) * STEP + (y >> 3)
    choose = jnp.where(col == wanted, 1.0, 0.0).astype(bf16)
    first = lax.div(lax.rem(z_first, PERIOD), DEEP)

    def natural(k):
        parts = []
        for i in range(4):
            h = lax.rem(first + 4 * k + i, GY)
            parts.append(in_ref[pl.ds(pl.multiple_of(h * group, group), group), :])
        made = lax.dot_general(
            choose, jnp.concatenate(parts, axis=0), (((1,), (1,)), ((), ())), preferred_element_type=f32
        )
        made_ref[:, pl.ds(k * 256, 256)] = made.astype(bf16)

    made_ref[:, pl.ds(GY * group, 128)] = jnp.zeros((YCAP, 128), bf16)
    source = lax.broadcasted_iota(jnp.int32, (WIDE, 256), 0)
    lane = lax.broadcasted_iota(jnp.int32, (WIDE, 256), 1)
    slot = (lane >> 3) + lax.rem(z_first, DEEP)
    wanted = (slot >> 3) * group + (lane & 7) * DEEP + (slot & 7)
    weave_ref[...] = jnp.where(source == wanted, 1.0, 0.0).astype(bf16)
    flat = X * ZCAP
    stores = []
    natural(0)
    for k in range(-(-flat // 256)):
        if k + 1 < GY // 4:
            natural(k + 1)
        wide = min(256, flat - 256 * k)
        span = pl.ds(k * 256, wide)
        planes = made_ref[:, pl.ds(k * 256, WIDE)]
        picked = jnp.dot(planes, weave_ref[...], preferred_element_type=f32)[:, :wide] * factor
        row = lax.broadcasted_iota(jnp.int32, (YCAP, wide), 0)
        slot = (lax.broadcasted_iota(jnp.int32, (YCAP, wide), 1) + k * 256) >> 3
        valid = (row < y_extent) & (slot < z_extent)
        vp_out_ref[:, span] = jnp.where(valid, vp_ref[:, span].astype(f32) * (1.0 + picked), 0.0)
        vs_out_ref[:, span] = jnp.where(valid, vs_ref[:, span].astype(f32) * (1.0 + picked), 0.0)
        rho_out_ref[:, span] = jnp.where(valid, rho_ref[:, span].astype(f32) * (1.0 + DENSITY_GAIN * picked), 0.0)
        pairs = ((vp_out_ref, new_vp_ref), (vs_out_ref, new_vs_ref), (rho_out_ref, new_rho_ref))
        for i, (a, b) in enumerate(pairs):
            stores.append(pltpu.make_async_copy(a.at[:, span], b.at[:, span], sem.at[i, k]))
            stores[-1].start()
    for store in stores:
        store.wait()


SMEM = pl.BlockSpec(memory_space=pltpu.SMEM)
VMEM = pl.BlockSpec(memory_space=pltpu.VMEM)
HBM = pl.BlockSpec(memory_space=pltpu.HBM)


def held(array):
    return pltpu.with_memory_space_constraint(array, pltpu.HBM)


def depth_stage(place, spec):
    return pl.pallas_call(
        depth_kernel,
        out_shape=pltpu.VMEM((GY, 2 * BAND, ROWS), bf16),
        in_specs=[SMEM, HBM, HBM, HBM],
        out_specs=VMEM,
        scratch_shapes=[
            pltpu.VMEM((2, ROWS, NZ), bf16),
            pltpu.VMEM((OUTER, ROWS, 2 * INNER), bf16),
            pltpu.VMEM((2, 2, NZ, 128), f32),
            pltpu.VMEM((2 * OUTER, INNER), f32),
            pltpu.VMEM((2 * INNER, 2 * INNER), bf16),
            pltpu.SemaphoreType.DMA((ROWS // CHUNK,)),
            pltpu.SemaphoreType.DMA((2,)),
        ],
        compiler_params=pltpu.CompilerParams(vmem_limit_bytes=32 * MIB),
    )(place, held(spec), held(jnp.asarray(depth_twist())), held(jnp.asarray(inner_table())))


def y_stage(place, y_bounds, z_bounds, turned, taper, *models):
    return pl.pallas_call(
        y_kernel,
        out_shape=[pltpu.VMEM((GY * GZ * DEEP, WIDE), bf16)] + [pltpu.VMEM(m.shape, bf16) for m in models],
        in_specs=[SMEM, SMEM, SMEM, VMEM, VMEM, VMEM, HBM, HBM, HBM, HBM],
        out_specs=[VMEM] * 4,
        scratch_shapes=[
            pltpu.VMEM((RADIX * BAND, 2 * LONG), bf16),
            pltpu.VMEM((LONG // 128, RADIX * BAND, 128), f32),
            pltpu.VMEM((MANY, TILES, BAND + DEEP, 128), f32),
            pltpu.VMEM((LONG // 256, 2 * LONG, 256), bf16),
            pltpu.SemaphoreType.DMA((3,)),
            pltpu.SemaphoreType.DMA((LONG // 256,)),
        ],
        compiler_params=pltpu.CompilerParams(vmem_limit_bytes=32 * MIB),
    )(place, y_bounds, z_bounds, turned, taper, y_twist(), held(jnp.asarray(y_table())), *[held(m) for m in models])


def model_stage(place, y_bounds, z_bounds, bricks, vp, vs, rho):
    flat = X * ZCAP
    whole = pltpu.VMEM((YCAP, flat), f32)
    return pl.pallas_call(
        model_kernel,
        out_shape=[jax.ShapeDtypeStruct((YCAP, flat), f32)] * 3,
        in_specs=[SMEM, SMEM, SMEM, VMEM, VMEM, VMEM, VMEM],
        out_specs=[HBM] * 3,
        scratch_shapes=[
            pltpu.VMEM((YCAP, GY * X * DEEP + 128), bf16),
            pltpu.VMEM((WIDE, 256), bf16),
            whole,
            whole,
            whole,
            pltpu.SemaphoreType.DMA((3, -(-flat // 256))),
        ],
        compiler_params=pltpu.CompilerParams(vmem_limit_bytes=32 * MIB),
    )(place, y_bounds, z_bounds, bricks, vp, vs, rho)


def shards(spectrum, layer_index, y_bounds, z_bounds, vp, vs, rho):
    gy_index = lax.axis_index("gy")
    place = jnp.stack([gy_index, lax.axis_index("gz")])
    taper_all = (layer_index.astype(f32) + 1.0) / LAYERS
    taper_band = lax.dynamic_index_in_dim(taper_all.reshape(BAND // DEEP, GY, DEEP), gy_index, 1, False).reshape(BAND)
    taper = jnp.broadcast_to(jnp.tile(taper_band, RADIX)[:, None], (RADIX * BAND, 128))
    turned = depth_stage(place, spectrum.reshape(2, ROWS, NZ))
    turned = lax.all_to_all(turned, "gy", 0, 0, tiled=True)
    bricks, *models = y_stage(place, y_bounds, z_bounds, turned, taper, vp, vs, rho)
    bricks = lax.all_to_all(bricks.reshape(GY * GZ, DEEP, WIDE), ("gy", "gz"), 0, 0, tiled=True)
    bricks = bricks.reshape(GY * X * DEEP, WIDE)
    return tuple(model_stage(place, y_bounds, z_bounds, bricks, *models))


def solution(mesh):
    return jax.shard_map(
        shards,
        mesh=mesh,
        in_specs=(
            P(None, "gz", "gy", None),
            P(),
            P(),
            P(),
            P("gy", "gz"),
            P("gy", "gz"),
            P("gy", "gz"),
        ),
        out_specs=(P("gy", "gz"), P("gy", "gz"), P("gy", "gz")),
        check_vma=False,
    )
```

```python
import functools
import math

import jax
import jax.numpy as jnp
import numpy as np
from jax import lax
from jax.experimental import pallas as pl
from jax.experimental.pallas import tpu as pltpu
from jax.sharding import PartitionSpec as P

LAYERS = 8
CORRELATION = 8.0
HURST_EXPONENT = 0.1
SPREAD_SIGMA = 0.1
DENSITY_GAIN = 0.8
EPSILON = 1e-06

NY, NZ, X = 8192, 1536, 8
GY, GZ = 32, 8
ROWS = NY // GY
CHUNK = 64
BAND = NZ // GY
YCAP, ZCAP = 320, 240
INNER = 128
OUTER = NZ // INNER
RADIX = 16
LONG = NY // RADIX
STEP = YCAP // RADIX + 1
PER = 6
WIDE = 384
MANY = 8
TILES = WIDE // 128
DEEP = 8
PERIOD = GY * DEEP
f32, bf16 = jnp.float32, jnp.bfloat16
MIB = 1024 * 1024


def inner_table():
    angle = 2.0 * np.pi * (np.outer(np.arange(INNER), np.arange(INNER)) % INNER) / INNER
    c, s = np.cos(angle), np.sin(angle)
    return np.block([[c, -s], [s, c]]).astype(bf16)


def depth_twist():
    angle = 2.0 * np.pi * np.outer(np.arange(OUTER), np.arange(INNER)) / NZ
    return np.stack([np.cos(angle), np.sin(angle)], axis=1).reshape(2 * OUTER, INNER).astype(np.float32)


def y_table():
    angle = 2.0 * np.pi * (np.outer(np.arange(LONG), np.arange(LONG)) % LONG) / LONG
    full = np.concatenate([np.cos(angle), -np.sin(angle)], axis=0).astype(bf16)
    return np.ascontiguousarray(full.reshape(2 * LONG, LONG // 256, 256).transpose(1, 0, 2))


def y_twist():
    y1 = np.arange(RADIX)
    angle = 2.0 * np.pi * np.outer(y1 - RADIX * STEP * (y1 % PER), np.arange(LONG)) / NY
    both = np.stack([np.cos(angle), np.sin(angle)], axis=1).astype(np.float32)
    split = both.reshape(2 * RADIX, LONG // ROWS, ROWS).transpose(1, 0, 2)
    return np.ascontiguousarray(split)


def four(a):
    (r0, i0), (r1, i1), (r2, i2), (r3, i3) = a
    sr, si, dr, di = r0 + r2, i0 + i2, r0 - r2, i0 - i2
    tr, ti, er, ei = r1 + r3, i1 + i3, r1 - r3, i1 - i3
    return [(sr + tr, si + ti), (dr - ei, di + er), (sr - tr, si - ti), (dr + ei, di - er)]


def three(a):
    (r0, i0), (r1, i1), (r2, i2) = a
    tr, ti = r1 + r2, i1 + i2
    half = math.sqrt(3.0) / 2.0
    er, ei = (r1 - r2) * half, (i1 - i2) * half
    mr, mi = r0 - 0.5 * tr, i0 - 0.5 * ti
    return [(r0 + tr, i0 + ti), (mr - ei, mi + er), (mr + ei, mi - er)]


def twelve(a):
    quarter = [four([a[(4 * i + 3 * j) % 12] for j in range(4)]) for i in range(3)]
    out = [None] * 12
    for v in range(4):
        for u, value in enumerate(three([quarter[i][v] for i in range(3)])):
            out[next(q for q in range(12) if q % 3 == u and q % 4 == v)] = value
    return out


def sixteen(a):
    first = []
    for b in range(4):
        column = four(a[b::4])
        for k in range(1, 4):
            if b:
                c, s = math.cos(math.pi * b * k / 8.0), math.sin(math.pi * b * k / 8.0)
                re, im = column[k]
                column[k] = (re * c - im * s, re * s + im * c)
        first.append(column)
    last = [four([first[b][k] for b in range(4)]) for k in range(4)]
    return [last[k % 4][k // 4] for k in range(16)]


def depth_kernel(
    spec_ref, twist_hbm_ref, table_hbm_ref, out_ref, rows_ref, mid_ref, hold_ref, twist_ref, table_ref, sem, table_sem
):
    first = lax.axis_index("gy") * ROWS
    lane = lax.broadcasted_iota(jnp.int32, (16, INNER), 1)
    line = lax.broadcasted_iota(jnp.int32, (16, INNER), 0)

    def load(k):
        rows = pl.ds(pl.multiple_of(k * CHUNK, CHUNK), CHUNK)
        return pltpu.make_async_copy(spec_ref.at[:, rows, :], rows_ref.at[:, rows, :], sem.at[k])

    fetches = [
        pltpu.make_async_copy(twist_hbm_ref, twist_ref, table_sem.at[0]),
        pltpu.make_async_copy(table_hbm_ref, table_ref, table_sem.at[1]),
    ]
    fetches[0].start()
    for k in range(ROWS // CHUNK):
        load(k).start()
    fetches[1].start()
    fetches[0].wait()

    def rows_at(step, carry):
        at = pl.multiple_of(step * 16, 16)
        ky = first + at + line
        wy = jnp.where(2 * ky < NY, ky, ky - NY).astype(f32) * (2.0 * math.pi / NY)
        wy2 = wy * wy
        values = []
        for p in range(OUTER):
            kz = lane + p * INNER
            wz = jnp.where(2 * kz < NZ, kz, kz - NZ).astype(f32) * (2.0 * math.pi / NZ)
            base = 1.0 + CORRELATION * CORRELATION * (wy2 + wz * wz)
            gain = jnp.exp(jnp.log(base) * (-(HURST_EXPONENT + 1.0) / 2.0)) * (1.0 / math.sqrt(NY * NZ))
            span = pl.ds(p * INNER, INNER)
            values.append(
                (
                    rows_ref[0, pl.ds(at, 16), span].astype(f32) * gain,
                    rows_ref[1, pl.ds(at, 16), span].astype(f32) * gain,
                )
            )
        for q, (re, im) in enumerate(twelve(values)):
            c = twist_ref[pl.ds(2 * q, 1), :]
            s = twist_ref[pl.ds(2 * q + 1, 1), :]
            mid_ref[q, pl.ds(at, 16), pl.ds(0, INNER)] = (re * c - im * s).astype(bf16)
            mid_ref[q, pl.ds(at, 16), pl.ds(INNER, INNER)] = (re * s + im * c).astype(bf16)
        return carry

    def chunk(k, carry):
        load(k).wait()
        for i in range(CHUNK // 16):
            rows_at(k * (CHUNK // 16) + i, carry)
        return carry

    lax.fori_loop(0, ROWS // CHUNK, chunk, 0)
    fetches[1].wait()
    for q in range(OUTER):
        made = lax.dot_general(
            table_ref[...], mid_ref[q], (((1,), (1,)), ((), ())), preferred_element_type=f32
        )
        for half in range(2):
            for part in range(2):
                hold_ref[half, part, pl.ds(q, INNER, stride=OUTER), :] = made[
                    part * INNER : (part + 1) * INNER, half * 128 : (half + 1) * 128
                ]

    def pack(h, carry):
        for part in range(2):
            for b in range(0, BAND // DEEP, 2):
                for half in range(2):
                    two = [
                        hold_ref[half, part, pl.ds(pl.multiple_of((b + i) * PERIOD + h * DEEP, DEEP), DEEP), :]
                        for i in range(2)
                    ]
                    to = pl.ds(part * BAND + b * DEEP, 2 * DEEP)
                    out_ref[h, to, pl.ds(half * 128, 128)] = jnp.concatenate(two, axis=0).astype(bf16)
        return carry

    lax.fori_loop(0, GY, pack, 0, unroll=4)


def pieces(value):
    high = value.astype(bf16).astype(f32)
    rest = value - high
    middle = rest.astype(bf16).astype(f32)
    return high, middle, rest - middle


def y_kernel(
    y_bounds_ref, z_bounds_ref, in_ref, taper_ref, twist_ref, wave_hbm_ref, vp_ref, vs_ref, rho_ref,
    out_ref, vp_out_ref, vs_out_ref, rho_out_ref, mid_ref, field_ref, cut_ref, wave_ref, sem, wave_sem
):
    groups = LONG // ROWS
    models = ((vp_ref, vp_out_ref), (vs_ref, vs_out_ref), (rho_ref, rho_out_ref))
    fetches = [pltpu.make_async_copy(a, b, sem.at[k]) for k, (a, b) in enumerate(models)]
    waves = [pltpu.make_async_copy(wave_hbm_ref.at[k], wave_ref.at[k], wave_sem.at[k]) for k in range(LONG // 256)]
    for wave in waves:
        wave.start()

    def turn(low, carry):
        for row in range(0, BAND, 16):
            for col in range(0, ROWS, 128):
                values = []
                for e in range(RADIX):
                    block = groups * e + low
                    values.append(
                        (
                            in_ref[block, pl.ds(row, 16), pl.ds(col, 128)].astype(f32),
                            in_ref[block, pl.ds(BAND + row, 16), pl.ds(col, 128)].astype(f32),
                        )
                    )
                lanes = pl.multiple_of(low * ROWS + col, 128)
                for y1, (re, im) in enumerate(sixteen(values)):
                    c = twist_ref[low, pl.ds(2 * y1, 1), pl.ds(col, 128)]
                    s = twist_ref[low, pl.ds(2 * y1 + 1, 1), pl.ds(col, 128)]
                    at = pl.ds(y1 * BAND + row, 16)
                    mid_ref[at, pl.ds(lanes, 128)] = (re * c - im * s).astype(bf16)
                    mid_ref[at, pl.ds(pl.multiple_of(lanes + LONG, 128), 128)] = (re * s + im * c).astype(bf16)
        return carry

    lax.fori_loop(0, groups, turn, 0)
    total = jnp.zeros((8, 128), f32)
    taper = taper_ref[...]
    for block in range(LONG // 256):
        waves[block].wait()
        if block == len(waves) - 1:
            for fetch in fetches:
                fetch.start()
        made = jnp.dot(mid_ref[...], wave_ref[block], preferred_element_type=f32)
        for half in range(2):
            part = made[:, half * 128 : (half + 1) * 128] * taper
            field_ref[2 * block + half] = part
            total = total + jnp.sum((part * part).reshape(RADIX * BAND // 8, 8, 128), axis=0)
    sums = jnp.sum(jnp.sum(total, axis=0, keepdims=True), axis=1, keepdims=True)
    high, middle, low = pieces(jnp.broadcast_to(sums, (BAND, 128)))
    lane = lax.broadcasted_iota(jnp.int32, (BAND, 128), 1)
    extra = jnp.where(lane == 125, high, jnp.where(lane == 126, middle, jnp.where(lane == 127, low, 0.0)))
    for i in range(MANY):
        cut_ref[i, :, pl.ds(BAND, DEEP), :] = jnp.zeros((TILES, DEEP, 128), f32)
        cut_ref[i, TILES - 1, pl.ds(BAND, DEEP), :] = extra[:DEEP]
    here = lax.axis_index("gy") * DEEP
    tiles = [lax.div(z_bounds_ref[j] - here + (PERIOD - DEEP), PERIOD) * DEEP for j in range(GZ)]

    def window(g, place):
        y2_first = lax.div(y_bounds_ref[g], RADIX)
        block = lax.div(y2_first, 128)
        later = lax.rem(block + 1, LONG // 128)
        shift = lax.rem(y2_first, 128)
        before = lane < shift
        at = lane - shift + jnp.where(before, 128, 0)
        cut = jnp.minimum(lax.div(127 - shift, STEP), PER - 1)
        split = before & (at < STEP * (cut + 1))
        blocks = [jnp.where(i > cut, later, block) for i in range(PER)]
        for tile in range(TILES):
            parts = []
            for y1 in range(tile * PER, min(tile * PER + PER, RADIX)):
                parts.append(field_ref[blocks[y1 % PER], pl.ds(y1 * BAND, BAND), :])
            whole = parts[-1]
            for i in reversed(range(len(parts) - 1)):
                whole = jnp.where(at < STEP * (i + 1), parts[i], whole)
            other = jnp.minimum(tile * PER + cut, RADIX - 1)
            rows = pl.ds(pl.multiple_of(other * BAND, BAND), BAND)
            whole = jnp.where(split, field_ref[later, rows, :], whole)
            whole = pltpu.roll(whole, lax.rem(128 - shift, 128), 1)
            if tile == TILES - 1:
                whole = jnp.where(lane < STEP * len(parts), whole, extra)
            cut_ref[place, tile, pl.ds(0, BAND), :] = whole

    def send(g, place):
        for j in range(0, GZ, 2):
            to = pl.ds(pl.multiple_of((g * GZ + j) * DEEP, 2 * DEEP), 2 * DEEP)
            for tile in range(TILES):
                two = [cut_ref[place, tile, pl.ds(pl.multiple_of(tiles[j + i], DEEP), DEEP), :] for i in range(2)]
                out_ref[to, pl.ds(tile * 128, 128)] = jnp.concatenate(two, axis=0).astype(bf16)

    def several(k, carry):
        for i in range(MANY):
            window(k * MANY + i, i)
        for i in range(MANY):
            send(k * MANY + i, i)
        return carry

    lax.fori_loop(0, GY // MANY, several, 0)
    for fetch in fetches:
        fetch.wait()


def model_kernel(
    y_bounds_ref, z_bounds_ref, in_ref, vp_ref, vs_ref, rho_ref, new_vp_ref, new_vs_ref, new_rho_ref,
    made_ref, weave_ref, vp_out_ref, vs_out_ref, rho_out_ref, sem
):
    row, col = lax.axis_index("gy"), lax.axis_index("gz")
    y_first = y_bounds_ref[row]
    y_extent = y_bounds_ref[row + 1] - y_first
    z_first = z_bounds_ref[col]
    z_extent = z_bounds_ref[col + 1] - z_first
    group = X * DEEP
    tail = jnp.zeros((16, 128), f32)
    for k in range(GY * X * DEEP // 16):
        tail = tail + in_ref[pl.ds(16 * k, 16), pl.ds(WIDE - 128, 128)].astype(f32)
    first_row = lax.broadcasted_iota(jnp.int32, (16, 128), 0) % DEEP == 0
    first_row = first_row & (lax.broadcasted_iota(jnp.int32, (16, 128), 1) >= 125)
    total = jnp.sum(jnp.where(first_row, tail, 0.0), axis=0, keepdims=True)
    total = jnp.sum(total, axis=1, keepdims=True)
    factor = SPREAD_SIGMA / jnp.sqrt(total / (X * NY * NZ) + EPSILON)
    r = lax.broadcasted_iota(jnp.int32, (YCAP, WIDE), 0)
    col = lax.broadcasted_iota(jnp.int32, (YCAP, WIDE), 1)
    y = r + lax.rem(y_first, RADIX)
    y1 = y & (RADIX - 1)
    third = jnp.where(y1 >= 2 * PER, 2, jnp.where(y1 >= PER, 1, 0))
    wanted = third * 128 + (y1 - PER * third) * STEP + lax.div(y, RADIX)
    choose = jnp.where(col == wanted, 1.0, 0.0).astype(bf16)
    first = lax.div(lax.rem(z_first, PERIOD), DEEP)

    def natural(k):
        parts = []
        for i in range(4):
            h = lax.rem(first + 4 * k + i, GY)
            parts.append(in_ref[pl.ds(pl.multiple_of(h * group, group), group), :])
        made = lax.dot_general(
            choose, jnp.concatenate(parts, axis=0), (((1,), (1,)), ((), ())), preferred_element_type=f32
        )
        made_ref[:, pl.ds(k * 256, 256)] = made.astype(bf16)

    made_ref[:, pl.ds(GY * group, 128)] = jnp.zeros((YCAP, 128), bf16)
    source = lax.broadcasted_iota(jnp.int32, (WIDE, 256), 0)
    lane = lax.broadcasted_iota(jnp.int32, (WIDE, 256), 1)
    slot = (lane >> 3) + lax.rem(z_first, DEEP)
    wanted = (slot >> 3) * group + (lane & 7) * DEEP + (slot & 7)
    weave_ref[...] = jnp.where(source == wanted, 1.0, 0.0).astype(bf16)
    flat = X * ZCAP
    stores = []
    natural(0)
    for k in range(-(-flat // 256)):
        if k + 1 < GY // 4:
            natural(k + 1)
        wide = min(256, flat - 256 * k)
        span = pl.ds(k * 256, wide)
        planes = made_ref[:, pl.ds(k * 256, WIDE)]
        picked = jnp.dot(planes, weave_ref[...], preferred_element_type=f32)[:, :wide] * factor
        row = lax.broadcasted_iota(jnp.int32, (YCAP, wide), 0)
        slot = (lax.broadcasted_iota(jnp.int32, (YCAP, wide), 1) + k * 256) >> 3
        valid = (row < y_extent) & (slot < z_extent)
        vp_out_ref[:, span] = jnp.where(valid, vp_ref[:, span].astype(f32) * (1.0 + picked), 0.0)
        vs_out_ref[:, span] = jnp.where(valid, vs_ref[:, span].astype(f32) * (1.0 + picked), 0.0)
        rho_out_ref[:, span] = jnp.where(valid, rho_ref[:, span].astype(f32) * (1.0 + DENSITY_GAIN * picked), 0.0)
        pairs = ((vp_out_ref, new_vp_ref), (vs_out_ref, new_vs_ref), (rho_out_ref, new_rho_ref))
        for i, (a, b) in enumerate(pairs):
            stores.append(pltpu.make_async_copy(a.at[:, span], b.at[:, span], sem.at[i, k]))
            stores[-1].start()
    for store in stores:
        store.wait()


SMEM = pl.BlockSpec(memory_space=pltpu.SMEM)
VMEM = pl.BlockSpec(memory_space=pltpu.VMEM)
HBM = pl.BlockSpec(memory_space=pltpu.HBM)


def held(array):
    return pltpu.with_memory_space_constraint(array, pltpu.HBM)


def depth_stage(spec):
    return pl.pallas_call(
        depth_kernel,
        out_shape=pltpu.VMEM((GY, 2 * BAND, ROWS), bf16),
        in_specs=[HBM, HBM, HBM],
        out_specs=VMEM,
        scratch_shapes=[
            pltpu.VMEM((2, ROWS, NZ), bf16),
            pltpu.VMEM((OUTER, ROWS, 2 * INNER), bf16),
            pltpu.VMEM((2, 2, NZ, 128), f32),
            pltpu.VMEM((2 * OUTER, INNER), f32),
            pltpu.VMEM((2 * INNER, 2 * INNER), bf16),
            pltpu.SemaphoreType.DMA((ROWS // CHUNK,)),
            pltpu.SemaphoreType.DMA((2,)),
        ],
        compiler_params=pltpu.CompilerParams(vmem_limit_bytes=32 * MIB),
    )(held(spec), held(jnp.asarray(depth_twist())), held(jnp.asarray(inner_table())))


def y_stage(y_bounds, z_bounds, turned, taper, *models):
    return pl.pallas_call(
        y_kernel,
        out_shape=[pltpu.VMEM((GY * GZ * DEEP, WIDE), bf16)] + [pltpu.VMEM(m.shape, bf16) for m in models],
        in_specs=[SMEM, SMEM, VMEM, VMEM, VMEM, HBM, HBM, HBM, HBM],
        out_specs=[VMEM] * 4,
        scratch_shapes=[
            pltpu.VMEM((RADIX * BAND, 2 * LONG), bf16),
            pltpu.VMEM((LONG // 128, RADIX * BAND, 128), f32),
            pltpu.VMEM((MANY, TILES, BAND + DEEP, 128), f32),
            pltpu.VMEM((LONG // 256, 2 * LONG, 256), bf16),
            pltpu.SemaphoreType.DMA((3,)),
            pltpu.SemaphoreType.DMA((LONG // 256,)),
        ],
        compiler_params=pltpu.CompilerParams(vmem_limit_bytes=32 * MIB),
    )(y_bounds, z_bounds, turned, taper, y_twist(), held(jnp.asarray(y_table())), *[held(m) for m in models])


def model_stage(y_bounds, z_bounds, bricks, vp, vs, rho):
    flat = X * ZCAP
    whole = pltpu.VMEM((YCAP, flat), f32)
    return pl.pallas_call(
        model_kernel,
        out_shape=[jax.ShapeDtypeStruct((YCAP, flat), f32)] * 3,
        in_specs=[SMEM, SMEM, VMEM, VMEM, VMEM, VMEM],
        out_specs=[HBM] * 3,
        scratch_shapes=[
            pltpu.VMEM((YCAP, GY * X * DEEP + 128), bf16),
            pltpu.VMEM((WIDE, 256), bf16),
            whole,
            whole,
            whole,
            pltpu.SemaphoreType.DMA((3, -(-flat // 256))),
        ],
        compiler_params=pltpu.CompilerParams(vmem_limit_bytes=32 * MIB),
    )(y_bounds, z_bounds, bricks, vp, vs, rho)


def shards(spectrum, layer_index, y_bounds, z_bounds, vp, vs, rho):
    gy_index = lax.axis_index("gy")
    taper_all = (layer_index.astype(f32) + 1.0) / LAYERS
    taper_band = lax.dynamic_index_in_dim(taper_all.reshape(BAND // DEEP, GY, DEEP), gy_index, 1, False).reshape(BAND)
    taper = jnp.broadcast_to(jnp.tile(taper_band, RADIX)[:, None], (RADIX * BAND, 128))
    turned = depth_stage(spectrum.reshape(2, ROWS, NZ))
    turned = lax.all_to_all(turned, "gy", 0, 0, tiled=True)
    bricks, *models = y_stage(y_bounds, z_bounds, turned, taper, vp, vs, rho)
    bricks = lax.all_to_all(bricks.reshape(GY * GZ, DEEP, WIDE), ("gy", "gz"), 0, 0, tiled=True)
    bricks = bricks.reshape(GY * X * DEEP, WIDE)
    return tuple(model_stage(y_bounds, z_bounds, bricks, *models))


def solution(mesh):
    return jax.shard_map(
        shards,
        mesh=mesh,
        in_specs=(
            P(None, "gz", "gy", None),
            P(),
            P(),
            P(),
            P("gy", "gz"),
            P("gy", "gz"),
            P("gy", "gz"),
        ),
        out_specs=(P("gy", "gz"), P("gy", "gz"), P("gy", "gz")),
        check_vma=False,
    )
```

```python
import functools
import math

import jax
import jax.numpy as jnp
import numpy as np
from jax import lax
from jax.experimental import pallas as pl
from jax.experimental.pallas import tpu as pltpu
from jax.sharding import PartitionSpec as P

LAYERS = 8
CORRELATION = 8.0
HURST_EXPONENT = 0.1
SPREAD_SIGMA = 0.1
DENSITY_GAIN = 0.8
EPSILON = 1e-06

NY, NZ, X = 8192, 1536, 8
GY, GZ = 32, 8
ROWS = NY // GY
CHUNK = 64
BAND = NZ // GY
YCAP, ZCAP = 320, 240
INNER = 128
OUTER = NZ // INNER
RADIX = 16
LONG = NY // RADIX
STEP = YCAP // RADIX + 1
PER = 6
WIDE = 384
MANY = 16
TILES = WIDE // 128
DEEP = 8
PERIOD = GY * DEEP
f32, bf16 = jnp.float32, jnp.bfloat16
MIB = 1024 * 1024


def inner_table():
    angle = 2.0 * np.pi * (np.outer(np.arange(INNER), np.arange(INNER)) % INNER) / INNER
    c, s = np.cos(angle), np.sin(angle)
    return np.block([[c, -s], [s, c]]).astype(bf16)


def depth_twist():
    angle = 2.0 * np.pi * np.outer(np.arange(OUTER), np.arange(INNER)) / NZ
    return np.stack([np.cos(angle), np.sin(angle)], axis=1).reshape(2 * OUTER, INNER).astype(np.float32)


def y_table():
    angle = 2.0 * np.pi * (np.outer(np.arange(LONG), np.arange(LONG)) % LONG) / LONG
    full = np.concatenate([np.cos(angle), -np.sin(angle)], axis=0).astype(bf16)
    return np.ascontiguousarray(full.reshape(2 * LONG, LONG // 256, 256).transpose(1, 0, 2))


def y_twist():
    y1 = np.arange(RADIX)
    angle = 2.0 * np.pi * np.outer(y1 - RADIX * STEP * (y1 % PER), np.arange(LONG)) / NY
    both = np.stack([np.cos(angle), np.sin(angle)], axis=1).astype(np.float32)
    split = both.reshape(2 * RADIX, LONG // ROWS, ROWS).transpose(1, 0, 2)
    return np.ascontiguousarray(split)


def four(a):
    (r0, i0), (r1, i1), (r2, i2), (r3, i3) = a
    sr, si, dr, di = r0 + r2, i0 + i2, r0 - r2, i0 - i2
    tr, ti, er, ei = r1 + r3, i1 + i3, r1 - r3, i1 - i3
    return [(sr + tr, si + ti), (dr - ei, di + er), (sr - tr, si - ti), (dr + ei, di - er)]


def three(a):
    (r0, i0), (r1, i1), (r2, i2) = a
    tr, ti = r1 + r2, i1 + i2
    half = math.sqrt(3.0) / 2.0
    er, ei = (r1 - r2) * half, (i1 - i2) * half
    mr, mi = r0 - 0.5 * tr, i0 - 0.5 * ti
    return [(r0 + tr, i0 + ti), (mr - ei, mi + er), (mr + ei, mi - er)]


def twelve(a):
    quarter = [four([a[(4 * i + 3 * j) % 12] for j in range(4)]) for i in range(3)]
    out = [None] * 12
    for v in range(4):
        for u, value in enumerate(three([quarter[i][v] for i in range(3)])):
            out[next(q for q in range(12) if q % 3 == u and q % 4 == v)] = value
    return out


def sixteen(a):
    first = []
    for b in range(4):
        column = four(a[b::4])
        for k in range(1, 4):
            if b:
                c, s = math.cos(math.pi * b * k / 8.0), math.sin(math.pi * b * k / 8.0)
                re, im = column[k]
                column[k] = (re * c - im * s, re * s + im * c)
        first.append(column)
    last = [four([first[b][k] for b in range(4)]) for k in range(4)]
    return [last[k % 4][k // 4] for k in range(16)]


def depth_kernel(
    spec_ref, twist_hbm_ref, table_hbm_ref, wave_ref, out_ref, wave_out_ref, rows_ref, mid_ref, hold_ref, twist_ref, table_ref, sem, table_sem
):
    first = lax.axis_index("gy") * ROWS
    lane = lax.broadcasted_iota(jnp.int32, (16, INNER), 1)
    line = lax.broadcasted_iota(jnp.int32, (16, INNER), 0)

    def load(k):
        rows = pl.ds(pl.multiple_of(k * CHUNK, CHUNK), CHUNK)
        return pltpu.make_async_copy(spec_ref.at[:, rows, :], rows_ref.at[:, rows, :], sem.at[k])

    fetches = [
        pltpu.make_async_copy(twist_hbm_ref, twist_ref, table_sem.at[0]),
        pltpu.make_async_copy(table_hbm_ref, table_ref, table_sem.at[1]),
        pltpu.make_async_copy(wave_ref, wave_out_ref, table_sem.at[2]),
    ]
    fetches[0].start()
    for k in range(ROWS // CHUNK):
        load(k).start()
    fetches[1].start()
    fetches[2].start()
    fetches[0].wait()

    def rows_at(step, carry):
        at = pl.multiple_of(step * 16, 16)
        ky = first + at + line
        wy = jnp.where(2 * ky < NY, ky, ky - NY).astype(f32) * (2.0 * math.pi / NY)
        wy2 = wy * wy
        values = []
        for p in range(OUTER):
            kz = lane + p * INNER
            wz = jnp.where(2 * kz < NZ, kz, kz - NZ).astype(f32) * (2.0 * math.pi / NZ)
            base = 1.0 + CORRELATION * CORRELATION * (wy2 + wz * wz)
            gain = jnp.exp(jnp.log(base) * (-(HURST_EXPONENT + 1.0) / 2.0)) * (1.0 / math.sqrt(NY * NZ))
            span = pl.ds(p * INNER, INNER)
            values.append(
                (
                    rows_ref[0, pl.ds(at, 16), span].astype(f32) * gain,
                    rows_ref[1, pl.ds(at, 16), span].astype(f32) * gain,
                )
            )
        for q, (re, im) in enumerate(twelve(values)):
            c = twist_ref[pl.ds(2 * q, 1), :]
            s = twist_ref[pl.ds(2 * q + 1, 1), :]
            mid_ref[q, pl.ds(at, 16), pl.ds(0, INNER)] = (re * c - im * s).astype(bf16)
            mid_ref[q, pl.ds(at, 16), pl.ds(INNER, INNER)] = (re * s + im * c).astype(bf16)
        return carry

    def chunk(k, carry):
        load(k).wait()
        for i in range(CHUNK // 16):
            rows_at(k * (CHUNK // 16) + i, carry)
        return carry

    lax.fori_loop(0, ROWS // CHUNK, chunk, 0)
    fetches[1].wait()
    for q in range(OUTER):
        made = lax.dot_general(
            table_ref[...], mid_ref[q], (((1,), (1,)), ((), ())), preferred_element_type=f32
        )
        for half in range(2):
            for part in range(2):
                hold_ref[half, part, pl.ds(q, INNER, stride=OUTER), :] = made[
                    part * INNER : (part + 1) * INNER, half * 128 : (half + 1) * 128
                ]

    def pack(h, carry):
        for part in range(2):
            for b in range(0, BAND // DEEP, 2):
                for half in range(2):
                    two = [
                        hold_ref[half, part, pl.ds(pl.multiple_of((b + i) * PERIOD + h * DEEP, DEEP), DEEP), :]
                        for i in range(2)
                    ]
                    to = pl.ds(part * BAND + b * DEEP, 2 * DEEP)
                    out_ref[h, to, pl.ds(half * 128, 128)] = jnp.concatenate(two, axis=0).astype(bf16)
        return carry

    lax.fori_loop(0, GY, pack, 0, unroll=4)
    fetches[2].wait()


def pieces(value):
    high = value.astype(bf16).astype(f32)
    rest = value - high
    middle = rest.astype(bf16).astype(f32)
    return high, middle, rest - middle


def y_kernel(
    y_bounds_ref, z_bounds_ref, in_ref, taper_ref, twist_ref, wave_ref, vp_ref, vs_ref, rho_ref,
    out_ref, vp_out_ref, vs_out_ref, rho_out_ref, mid_ref, field_ref, cut_ref, sem
):
    groups = LONG // ROWS
    models = ((vp_ref, vp_out_ref), (vs_ref, vs_out_ref), (rho_ref, rho_out_ref))
    fetches = [pltpu.make_async_copy(a, b, sem.at[k]) for k, (a, b) in enumerate(models)]
    for fetch in fetches:
        fetch.start()

    def turn(low, carry):
        for row in range(0, BAND, 16):
            for col in range(0, ROWS, 128):
                values = []
                for e in range(RADIX):
                    block = groups * e + low
                    values.append(
                        (
                            in_ref[block, pl.ds(row, 16), pl.ds(col, 128)].astype(f32),
                            in_ref[block, pl.ds(BAND + row, 16), pl.ds(col, 128)].astype(f32),
                        )
                    )
                lanes = pl.multiple_of(low * ROWS + col, 128)
                for y1, (re, im) in enumerate(sixteen(values)):
                    c = twist_ref[low, pl.ds(2 * y1, 1), pl.ds(col, 128)]
                    s = twist_ref[low, pl.ds(2 * y1 + 1, 1), pl.ds(col, 128)]
                    at = pl.ds(y1 * BAND + row, 16)
                    mid_ref[at, pl.ds(lanes, 128)] = (re * c - im * s).astype(bf16)
                    mid_ref[at, pl.ds(pl.multiple_of(lanes + LONG, 128), 128)] = (re * s + im * c).astype(bf16)
        return carry

    lax.fori_loop(0, groups, turn, 0)
    total = jnp.zeros((8, 128), f32)
    taper = taper_ref[...]
    for block in range(LONG // 256):
        made = jnp.dot(mid_ref[...], wave_ref[block], preferred_element_type=f32)
        for half in range(2):
            part = made[:, half * 128 : (half + 1) * 128] * taper
            field_ref[2 * block + half] = part
            total = total + jnp.sum((part * part).reshape(RADIX * BAND // 8, 8, 128), axis=0)
    sums = jnp.sum(jnp.sum(total, axis=0, keepdims=True), axis=1, keepdims=True)
    high, middle, low = pieces(jnp.broadcast_to(sums, (BAND, 128)))
    lane = lax.broadcasted_iota(jnp.int32, (BAND, 128), 1)
    extra = jnp.where(lane == 125, high, jnp.where(lane == 126, middle, jnp.where(lane == 127, low, 0.0)))
    for i in range(MANY):
        cut_ref[i, :, pl.ds(BAND, DEEP), :] = jnp.zeros((TILES, DEEP, 128), f32)
        cut_ref[i, TILES - 1, pl.ds(BAND, DEEP), :] = extra[:DEEP]
    here = lax.axis_index("gy") * DEEP
    tiles = [lax.div(z_bounds_ref[j] - here + (PERIOD - DEEP), PERIOD) * DEEP for j in range(GZ)]

    def window(g, place):
        y2_first = lax.div(y_bounds_ref[g], RADIX)
        block = lax.div(y2_first, 128)
        later = lax.rem(block + 1, LONG // 128)
        shift = lax.rem(y2_first, 128)
        before = lane < shift
        at = lane - shift + jnp.where(before, 128, 0)
        cut = jnp.minimum(lax.div(127 - shift, STEP), PER - 1)
        split = before & (at < STEP * (cut + 1))
        blocks = [jnp.where(i > cut, later, block) for i in range(PER)]
        for tile in range(TILES):
            parts = []
            for y1 in range(tile * PER, min(tile * PER + PER, RADIX)):
                parts.append(field_ref[blocks[y1 % PER], pl.ds(y1 * BAND, BAND), :])
            whole = parts[-1]
            for i in reversed(range(len(parts) - 1)):
                whole = jnp.where(at < STEP * (i + 1), parts[i], whole)
            other = jnp.minimum(tile * PER + cut, RADIX - 1)
            rows = pl.ds(pl.multiple_of(other * BAND, BAND), BAND)
            whole = jnp.where(split, field_ref[later, rows, :], whole)
            whole = pltpu.roll(whole, lax.rem(128 - shift, 128), 1)
            if tile == TILES - 1:
                whole = jnp.where(lane < STEP * len(parts), whole, extra)
            cut_ref[place, tile, pl.ds(0, BAND), :] = whole

    def send(g, place):
        for j in range(0, GZ, 2):
            to = pl.ds(pl.multiple_of((g * GZ + j) * DEEP, 2 * DEEP), 2 * DEEP)
            for tile in range(TILES):
                two = [cut_ref[place, tile, pl.ds(pl.multiple_of(tiles[j + i], DEEP), DEEP), :] for i in range(2)]
                out_ref[to, pl.ds(tile * 128, 128)] = jnp.concatenate(two, axis=0).astype(bf16)

    def several(k, carry):
        for i in range(MANY):
            window(k * MANY + i, i)
        for i in range(MANY):
            send(k * MANY + i, i)
        return carry

    lax.fori_loop(0, GY // MANY, several, 0)
    for fetch in fetches:
        fetch.wait()


def model_kernel(
    y_bounds_ref, z_bounds_ref, in_ref, vp_ref, vs_ref, rho_ref, new_vp_ref, new_vs_ref, new_rho_ref,
    made_ref, weave_ref, vp_out_ref, vs_out_ref, rho_out_ref, sem
):
    row, col = lax.axis_index("gy"), lax.axis_index("gz")
    y_first = y_bounds_ref[row]
    y_extent = y_bounds_ref[row + 1] - y_first
    z_first = z_bounds_ref[col]
    z_extent = z_bounds_ref[col + 1] - z_first
    group = X * DEEP
    tail = jnp.zeros((16, 128), f32)
    for k in range(GY * X * DEEP // 16):
        tail = tail + in_ref[pl.ds(16 * k, 16), pl.ds(WIDE - 128, 128)].astype(f32)
    first_row = lax.broadcasted_iota(jnp.int32, (16, 128), 0) % DEEP == 0
    first_row = first_row & (lax.broadcasted_iota(jnp.int32, (16, 128), 1) >= 125)
    total = jnp.sum(jnp.where(first_row, tail, 0.0), axis=0, keepdims=True)
    total = jnp.sum(total, axis=1, keepdims=True)
    factor = SPREAD_SIGMA / jnp.sqrt(total / (X * NY * NZ) + EPSILON)
    r = lax.broadcasted_iota(jnp.int32, (YCAP, WIDE), 0)
    col = lax.broadcasted_iota(jnp.int32, (YCAP, WIDE), 1)
    y = r + lax.rem(y_first, RADIX)
    y1 = y & (RADIX - 1)
    third = jnp.where(y1 >= 2 * PER, 2, jnp.where(y1 >= PER, 1, 0))
    wanted = third * 128 + (y1 - PER * third) * STEP + lax.div(y, RADIX)
    choose = jnp.where(col == wanted, 1.0, 0.0).astype(bf16)
    first = lax.div(lax.rem(z_first, PERIOD), DEEP)

    def natural(k):
        parts = []
        for i in range(4):
            h = lax.rem(first + 4 * k + i, GY)
            parts.append(in_ref[pl.ds(pl.multiple_of(h * group, group), group), :])
        made = lax.dot_general(
            choose, jnp.concatenate(parts, axis=0), (((1,), (1,)), ((), ())), preferred_element_type=f32
        )
        made_ref[:, pl.ds(k * 256, 256)] = made.astype(bf16)

    made_ref[:, pl.ds(GY * group, 128)] = jnp.zeros((YCAP, 128), bf16)
    source = lax.broadcasted_iota(jnp.int32, (WIDE, 256), 0)
    lane = lax.broadcasted_iota(jnp.int32, (WIDE, 256), 1)
    slot = (lane >> 3) + lax.rem(z_first, DEEP)
    wanted = (slot >> 3) * group + (lane & 7) * DEEP + (slot & 7)
    weave_ref[...] = jnp.where(source == wanted, 1.0, 0.0).astype(bf16)
    flat = X * ZCAP
    stores = []
    natural(0)
    for k in range(-(-flat // 256)):
        if k + 1 < GY // 4:
            natural(k + 1)
        wide = min(256, flat - 256 * k)
        span = pl.ds(k * 256, wide)
        planes = made_ref[:, pl.ds(k * 256, WIDE)]
        picked = jnp.dot(planes, weave_ref[...], preferred_element_type=f32)[:, :wide] * factor
        row = lax.broadcasted_iota(jnp.int32, (YCAP, wide), 0)
        slot = (lax.broadcasted_iota(jnp.int32, (YCAP, wide), 1) + k * 256) >> 3
        valid = (row < y_extent) & (slot < z_extent)
        vp_out_ref[:, span] = jnp.where(valid, vp_ref[:, span].astype(f32) * (1.0 + picked), 0.0)
        vs_out_ref[:, span] = jnp.where(valid, vs_ref[:, span].astype(f32) * (1.0 + picked), 0.0)
        rho_out_ref[:, span] = jnp.where(valid, rho_ref[:, span].astype(f32) * (1.0 + DENSITY_GAIN * picked), 0.0)
        pairs = ((vp_out_ref, new_vp_ref), (vs_out_ref, new_vs_ref), (rho_out_ref, new_rho_ref))
        for i, (a, b) in enumerate(pairs):
            stores.append(pltpu.make_async_copy(a.at[:, span], b.at[:, span], sem.at[i, k]))
            stores[-1].start()
    for store in stores:
        store.wait()


SMEM = pl.BlockSpec(memory_space=pltpu.SMEM)
VMEM = pl.BlockSpec(memory_space=pltpu.VMEM)
HBM = pl.BlockSpec(memory_space=pltpu.HBM)


def held(array):
    return pltpu.with_memory_space_constraint(array, pltpu.HBM)


def depth_stage(spec, wave):
    return pl.pallas_call(
        depth_kernel,
        out_shape=[pltpu.VMEM((GY, 2 * BAND, ROWS), bf16), pltpu.VMEM(wave.shape, bf16)],
        in_specs=[HBM, HBM, HBM, HBM],
        out_specs=[VMEM, VMEM],
        scratch_shapes=[
            pltpu.VMEM((2, ROWS, NZ), bf16),
            pltpu.VMEM((OUTER, ROWS, 2 * INNER), bf16),
            pltpu.VMEM((2, 2, NZ, 128), f32),
            pltpu.VMEM((2 * OUTER, INNER), f32),
            pltpu.VMEM((2 * INNER, 2 * INNER), bf16),
            pltpu.SemaphoreType.DMA((ROWS // CHUNK,)),
            pltpu.SemaphoreType.DMA((3,)),
        ],
        compiler_params=pltpu.CompilerParams(vmem_limit_bytes=32 * MIB),
    )(held(spec), held(jnp.asarray(depth_twist())), held(jnp.asarray(inner_table())), held(wave))


def y_stage(y_bounds, z_bounds, turned, taper, wave, *models):
    return pl.pallas_call(
        y_kernel,
        out_shape=[pltpu.VMEM((GY * GZ * DEEP, WIDE), bf16)] + [pltpu.VMEM(m.shape, bf16) for m in models],
        in_specs=[SMEM, SMEM, VMEM, VMEM, VMEM, VMEM, HBM, HBM, HBM],
        out_specs=[VMEM] * 4,
        scratch_shapes=[
            pltpu.VMEM((RADIX * BAND, 2 * LONG), bf16),
            pltpu.VMEM((LONG // 128, RADIX * BAND, 128), f32),
            pltpu.VMEM((MANY, TILES, BAND + DEEP, 128), f32),
            pltpu.SemaphoreType.DMA((3,)),
        ],
        compiler_params=pltpu.CompilerParams(vmem_limit_bytes=32 * MIB),
    )(y_bounds, z_bounds, turned, taper, y_twist(), wave, *[held(m) for m in models])


def model_stage(y_bounds, z_bounds, bricks, vp, vs, rho):
    flat = X * ZCAP
    whole = pltpu.VMEM((YCAP, flat), f32)
    return pl.pallas_call(
        model_kernel,
        out_shape=[jax.ShapeDtypeStruct((YCAP, flat), f32)] * 3,
        in_specs=[SMEM, SMEM, VMEM, VMEM, VMEM, VMEM],
        out_specs=[HBM] * 3,
        scratch_shapes=[
            pltpu.VMEM((YCAP, GY * X * DEEP + 128), bf16),
            pltpu.VMEM((WIDE, 256), bf16),
            whole,
            whole,
            whole,
            pltpu.SemaphoreType.DMA((3, -(-flat // 256))),
        ],
        compiler_params=pltpu.CompilerParams(vmem_limit_bytes=32 * MIB),
    )(y_bounds, z_bounds, bricks, vp, vs, rho)


def shards(spectrum, layer_index, y_bounds, z_bounds, vp, vs, rho):
    gy_index = lax.axis_index("gy")
    taper_all = (layer_index.astype(f32) + 1.0) / LAYERS
    taper_band = lax.dynamic_index_in_dim(taper_all.reshape(BAND // DEEP, GY, DEEP), gy_index, 1, False).reshape(BAND)
    taper = jnp.broadcast_to(jnp.tile(taper_band, RADIX)[:, None], (RADIX * BAND, 128))
    turned, wave = depth_stage(spectrum.reshape(2, ROWS, NZ), jnp.asarray(y_table()))
    turned = lax.all_to_all(turned, "gy", 0, 0, tiled=True)
    bricks, *models = y_stage(y_bounds, z_bounds, turned, taper, wave, vp, vs, rho)
    bricks = lax.all_to_all(bricks.reshape(GY * GZ, DEEP, WIDE), ("gy", "gz"), 0, 0, tiled=True)
    bricks = bricks.reshape(GY * X * DEEP, WIDE)
    return tuple(model_stage(y_bounds, z_bounds, bricks, *models))


def solution(mesh):
    return jax.shard_map(
        shards,
        mesh=mesh,
        in_specs=(
            P(None, "gz", "gy", None),
            P(),
            P(),
            P(),
            P("gy", "gz"),
            P("gy", "gz"),
            P("gy", "gz"),
        ),
        out_specs=(P("gy", "gz"), P("gy", "gz"), P("gy", "gz")),
        check_vma=False,
    )
```

```python
import functools
import math

import jax
import jax.numpy as jnp
import numpy as np
from jax import lax
from jax.experimental import pallas as pl
from jax.experimental.pallas import tpu as pltpu
from jax.sharding import PartitionSpec as P

LAYERS = 8
CORRELATION = 8.0
HURST_EXPONENT = 0.1
SPREAD_SIGMA = 0.1
DENSITY_GAIN = 0.8
EPSILON = 1e-06

NY, NZ, X = 8192, 1536, 8
GY, GZ = 32, 8
ROWS = NY // GY
CHUNK = 64
BAND = NZ // GY
YCAP, ZCAP = 320, 240
INNER = 128
OUTER = NZ // INNER
RADIX = 16
LONG = NY // RADIX
STEP = YCAP // RADIX + 1
PER = 6
WIDE = 384
MANY = 16
TILES = WIDE // 128
DEEP = 8
PERIOD = GY * DEEP
f32, bf16 = jnp.float32, jnp.bfloat16
MIB = 1024 * 1024


def inner_table():
    angle = 2.0 * np.pi * (np.outer(np.arange(INNER), np.arange(INNER)) % INNER) / INNER
    c, s = np.cos(angle), np.sin(angle)
    return np.block([[c, -s], [s, c]]).astype(bf16)


def depth_twist():
    angle = 2.0 * np.pi * np.outer(np.arange(OUTER), np.arange(INNER)) / NZ
    return np.stack([np.cos(angle), np.sin(angle)], axis=1).reshape(2 * OUTER, INNER).astype(np.float32)


def y_table():
    angle = 2.0 * np.pi * (np.outer(np.arange(LONG), np.arange(LONG)) % LONG) / LONG
    full = np.concatenate([np.cos(angle), -np.sin(angle)], axis=0).astype(bf16)
    return np.ascontiguousarray(full.reshape(2 * LONG, LONG // 256, 256).transpose(1, 0, 2))


def y_twist():
    y1 = np.arange(RADIX)
    angle = 2.0 * np.pi * np.outer(y1 - RADIX * STEP * (y1 % PER), np.arange(LONG)) / NY
    both = np.stack([np.cos(angle), np.sin(angle)], axis=1).astype(np.float32)
    split = both.reshape(2 * RADIX, LONG // ROWS, ROWS).transpose(1, 0, 2)
    return np.ascontiguousarray(split)


def four(a):
    (r0, i0), (r1, i1), (r2, i2), (r3, i3) = a
    sr, si, dr, di = r0 + r2, i0 + i2, r0 - r2, i0 - i2
    tr, ti, er, ei = r1 + r3, i1 + i3, r1 - r3, i1 - i3
    return [(sr + tr, si + ti), (dr - ei, di + er), (sr - tr, si - ti), (dr + ei, di - er)]


def three(a):
    (r0, i0), (r1, i1), (r2, i2) = a
    tr, ti = r1 + r2, i1 + i2
    half = math.sqrt(3.0) / 2.0
    er, ei = (r1 - r2) * half, (i1 - i2) * half
    mr, mi = r0 - 0.5 * tr, i0 - 0.5 * ti
    return [(r0 + tr, i0 + ti), (mr - ei, mi + er), (mr + ei, mi - er)]


def twelve(a):
    quarter = [four([a[(4 * i + 3 * j) % 12] for j in range(4)]) for i in range(3)]
    out = [None] * 12
    for v in range(4):
        for u, value in enumerate(three([quarter[i][v] for i in range(3)])):
            out[next(q for q in range(12) if q % 3 == u and q % 4 == v)] = value
    return out


def sixteen(a):
    first = []
    for b in range(4):
        column = four(a[b::4])
        for k in range(1, 4):
            if b:
                c, s = math.cos(math.pi * b * k / 8.0), math.sin(math.pi * b * k / 8.0)
                re, im = column[k]
                column[k] = (re * c - im * s, re * s + im * c)
        first.append(column)
    last = [four([first[b][k] for b in range(4)]) for k in range(4)]
    return [last[k % 4][k // 4] for k in range(16)]


def depth_kernel(
    spec_ref, twist_hbm_ref, table_hbm_ref, wave_ref, out_ref, wave_out_ref, rows_ref, mid_ref, hold_ref, twist_ref, table_ref, sem, table_sem
):
    first = lax.axis_index("gy") * ROWS
    lane = lax.broadcasted_iota(jnp.int32, (16, INNER), 1)
    line = lax.broadcasted_iota(jnp.int32, (16, INNER), 0)

    def load(k):
        rows = pl.ds(pl.multiple_of(k * CHUNK, CHUNK), CHUNK)
        return pltpu.make_async_copy(spec_ref.at[:, rows, :], rows_ref.at[:, rows, :], sem.at[k])

    fetches = [
        pltpu.make_async_copy(twist_hbm_ref, twist_ref, table_sem.at[0]),
        pltpu.make_async_copy(table_hbm_ref, table_ref, table_sem.at[1]),
        pltpu.make_async_copy(wave_ref, wave_out_ref, table_sem.at[2]),
    ]
    fetches[0].start()
    for k in range(ROWS // CHUNK):
        load(k).start()
    fetches[1].start()
    fetches[0].wait()

    def rows_at(step, carry):
        at = pl.multiple_of(step * 16, 16)
        ky = first + at + line
        wy = jnp.where(2 * ky < NY, ky, ky - NY).astype(f32) * (2.0 * math.pi / NY)
        wy2 = wy * wy
        values = []
        for p in range(OUTER):
            kz = lane + p * INNER
            wz = jnp.where(2 * kz < NZ, kz, kz - NZ).astype(f32) * (2.0 * math.pi / NZ)
            base = 1.0 + CORRELATION * CORRELATION * (wy2 + wz * wz)
            gain = jnp.exp(jnp.log(base) * (-(HURST_EXPONENT + 1.0) / 2.0)) * (1.0 / math.sqrt(NY * NZ))
            span = pl.ds(p * INNER, INNER)
            values.append(
                (
                    rows_ref[0, pl.ds(at, 16), span].astype(f32) * gain,
                    rows_ref[1, pl.ds(at, 16), span].astype(f32) * gain,
                )
            )
        for q, (re, im) in enumerate(twelve(values)):
            c = twist_ref[pl.ds(2 * q, 1), :]
            s = twist_ref[pl.ds(2 * q + 1, 1), :]
            mid_ref[q, pl.ds(at, 16), pl.ds(0, INNER)] = (re * c - im * s).astype(bf16)
            mid_ref[q, pl.ds(at, 16), pl.ds(INNER, INNER)] = (re * s + im * c).astype(bf16)
        return carry

    def chunk(k, carry):
        load(k).wait()
        for i in range(CHUNK // 16):
            rows_at(k * (CHUNK // 16) + i, carry)
        return carry

    lax.fori_loop(0, ROWS // CHUNK, chunk, 0)
    fetches[2].start()
    fetches[1].wait()
    for q in range(OUTER):
        made = lax.dot_general(
            table_ref[...], mid_ref[q], (((1,), (1,)), ((), ())), preferred_element_type=f32
        )
        for half in range(2):
            for part in range(2):
                hold_ref[half, part, pl.ds(q, INNER, stride=OUTER), :] = made[
                    part * INNER : (part + 1) * INNER, half * 128 : (half + 1) * 128
                ]

    def pack(h, carry):
        for part in range(2):
            for b in range(0, BAND // DEEP, 2):
                for half in range(2):
                    two = [
                        hold_ref[half, part, pl.ds(pl.multiple_of((b + i) * PERIOD + h * DEEP, DEEP), DEEP), :]
                        for i in range(2)
                    ]
                    to = pl.ds(part * BAND + b * DEEP, 2 * DEEP)
                    out_ref[h, to, pl.ds(half * 128, 128)] = jnp.concatenate(two, axis=0).astype(bf16)
        return carry

    lax.fori_loop(0, GY, pack, 0, unroll=4)
    fetches[2].wait()


def pieces(value):
    high = value.astype(bf16).astype(f32)
    rest = value - high
    middle = rest.astype(bf16).astype(f32)
    return high, middle, rest - middle


def y_kernel(
    y_bounds_ref, z_bounds_ref, in_ref, taper_ref, twist_ref, wave_ref, vp_ref, vs_ref, rho_ref,
    out_ref, vp_out_ref, vs_out_ref, rho_out_ref, mid_ref, field_ref, cut_ref, sem
):
    groups = LONG // ROWS
    models = ((vp_ref, vp_out_ref), (vs_ref, vs_out_ref), (rho_ref, rho_out_ref))
    fetches = [pltpu.make_async_copy(a, b, sem.at[k]) for k, (a, b) in enumerate(models)]
    for fetch in fetches:
        fetch.start()

    def turn(low, carry):
        for row in range(0, BAND, 16):
            for col in range(0, ROWS, 128):
                values = []
                for e in range(RADIX):
                    block = groups * e + low
                    values.append(
                        (
                            in_ref[block, pl.ds(row, 16), pl.ds(col, 128)].astype(f32),
                            in_ref[block, pl.ds(BAND + row, 16), pl.ds(col, 128)].astype(f32),
                        )
                    )
                lanes = pl.multiple_of(low * ROWS + col, 128)
                for y1, (re, im) in enumerate(sixteen(values)):
                    c = twist_ref[low, pl.ds(2 * y1, 1), pl.ds(col, 128)]
                    s = twist_ref[low, pl.ds(2 * y1 + 1, 1), pl.ds(col, 128)]
                    at = pl.ds(y1 * BAND + row, 16)
                    mid_ref[at, pl.ds(lanes, 128)] = (re * c - im * s).astype(bf16)
                    mid_ref[at, pl.ds(pl.multiple_of(lanes + LONG, 128), 128)] = (re * s + im * c).astype(bf16)
        return carry

    lax.fori_loop(0, groups, turn, 0)
    total = jnp.zeros((8, 128), f32)
    taper = taper_ref[...]
    for block in range(LONG // 256):
        made = jnp.dot(mid_ref[...], wave_ref[block], preferred_element_type=f32)
        for half in range(2):
            part = made[:, half * 128 : (half + 1) * 128] * taper
            field_ref[2 * block + half] = part
            total = total + jnp.sum((part * part).reshape(RADIX * BAND // 8, 8, 128), axis=0)
    sums = jnp.sum(jnp.sum(total, axis=0, keepdims=True), axis=1, keepdims=True)
    high, middle, low = pieces(jnp.broadcast_to(sums, (BAND, 128)))
    lane = lax.broadcasted_iota(jnp.int32, (BAND, 128), 1)
    extra = jnp.where(lane == 125, high, jnp.where(lane == 126, middle, jnp.where(lane == 127, low, 0.0)))
    for i in range(MANY):
        cut_ref[i, :, pl.ds(BAND, DEEP), :] = jnp.zeros((TILES, DEEP, 128), f32)
        cut_ref[i, TILES - 1, pl.ds(BAND, DEEP), :] = extra[:DEEP]
    here = lax.axis_index("gy") * DEEP
    tiles = [lax.div(z_bounds_ref[j] - here + (PERIOD - DEEP), PERIOD) * DEEP for j in range(GZ)]

    def window(g, place):
        y2_first = lax.div(y_bounds_ref[g], RADIX)
        block = lax.div(y2_first, 128)
        later = lax.rem(block + 1, LONG // 128)
        shift = lax.rem(y2_first, 128)
        before = lane < shift
        at = lane - shift + jnp.where(before, 128, 0)
        cut = jnp.minimum(lax.div(127 - shift, STEP), PER - 1)
        split = before & (at < STEP * (cut + 1))
        blocks = [jnp.where(i > cut, later, block) for i in range(PER)]
        for tile in range(TILES):
            parts = []
            for y1 in range(tile * PER, min(tile * PER + PER, RADIX)):
                parts.append(field_ref[blocks[y1 % PER], pl.ds(y1 * BAND, BAND), :])
            whole = parts[-1]
            for i in reversed(range(len(parts) - 1)):
                whole = jnp.where(at < STEP * (i + 1), parts[i], whole)
            other = jnp.minimum(tile * PER + cut, RADIX - 1)
            rows = pl.ds(pl.multiple_of(other * BAND, BAND), BAND)
            whole = jnp.where(split, field_ref[later, rows, :], whole)
            whole = pltpu.roll(whole, lax.rem(128 - shift, 128), 1)
            if tile == TILES - 1:
                whole = jnp.where(lane < STEP * len(parts), whole, extra)
            cut_ref[place, tile, pl.ds(0, BAND), :] = whole

    def send(g, place):
        for j in range(0, GZ, 2):
            to = pl.ds(pl.multiple_of((g * GZ + j) * DEEP, 2 * DEEP), 2 * DEEP)
            for tile in range(TILES):
                two = [cut_ref[place, tile, pl.ds(pl.multiple_of(tiles[j + i], DEEP), DEEP), :] for i in range(2)]
                out_ref[to, pl.ds(tile * 128, 128)] = jnp.concatenate(two, axis=0).astype(bf16)

    def several(k, carry):
        for i in range(MANY):
            window(k * MANY + i, i)
        for i in range(MANY):
            send(k * MANY + i, i)
        return carry

    lax.fori_loop(0, GY // MANY, several, 0)
    for fetch in fetches:
        fetch.wait()


def model_kernel(
    y_bounds_ref, z_bounds_ref, in_ref, vp_ref, vs_ref, rho_ref, new_vp_ref, new_vs_ref, new_rho_ref,
    made_ref, weave_ref, vp_out_ref, vs_out_ref, rho_out_ref, sem
):
    row, col = lax.axis_index("gy"), lax.axis_index("gz")
    y_first = y_bounds_ref[row]
    y_extent = y_bounds_ref[row + 1] - y_first
    z_first = z_bounds_ref[col]
    z_extent = z_bounds_ref[col + 1] - z_first
    group = X * DEEP
    tail = jnp.zeros((16, 128), f32)
    for k in range(GY * X * DEEP // 16):
        tail = tail + in_ref[pl.ds(16 * k, 16), pl.ds(WIDE - 128, 128)].astype(f32)
    first_row = lax.broadcasted_iota(jnp.int32, (16, 128), 0) % DEEP == 0
    first_row = first_row & (lax.broadcasted_iota(jnp.int32, (16, 128), 1) >= 125)
    total = jnp.sum(jnp.where(first_row, tail, 0.0), axis=0, keepdims=True)
    total = jnp.sum(total, axis=1, keepdims=True)
    factor = SPREAD_SIGMA / jnp.sqrt(total / (X * NY * NZ) + EPSILON)
    r = lax.broadcasted_iota(jnp.int32, (YCAP, WIDE), 0)
    col = lax.broadcasted_iota(jnp.int32, (YCAP, WIDE), 1)
    y = r + lax.rem(y_first, RADIX)
    y1 = y & (RADIX - 1)
    third = jnp.where(y1 >= 2 * PER, 2, jnp.where(y1 >= PER, 1, 0))
    wanted = third * 128 + (y1 - PER * third) * STEP + lax.div(y, RADIX)
    choose = jnp.where(col == wanted, 1.0, 0.0).astype(bf16)
    first = lax.div(lax.rem(z_first, PERIOD), DEEP)

    def natural(k):
        parts = []
        for i in range(4):
            h = lax.rem(first + 4 * k + i, GY)
            parts.append(in_ref[pl.ds(pl.multiple_of(h * group, group), group), :])
        made = lax.dot_general(
            choose, jnp.concatenate(parts, axis=0), (((1,), (1,)), ((), ())), preferred_element_type=f32
        )
        made_ref[:, pl.ds(k * 256, 256)] = made.astype(bf16)

    made_ref[:, pl.ds(GY * group, 128)] = jnp.zeros((YCAP, 128), bf16)
    source = lax.broadcasted_iota(jnp.int32, (WIDE, 256), 0)
    lane = lax.broadcasted_iota(jnp.int32, (WIDE, 256), 1)
    slot = (lane >> 3) + lax.rem(z_first, DEEP)
    wanted = (slot >> 3) * group + (lane & 7) * DEEP + (slot & 7)
    weave_ref[...] = jnp.where(source == wanted, 1.0, 0.0).astype(bf16)
    flat = X * ZCAP
    stores = []
    natural(0)
    for k in range(-(-flat // 256)):
        if k + 1 < GY // 4:
            natural(k + 1)
        wide = min(256, flat - 256 * k)
        span = pl.ds(k * 256, wide)
        planes = made_ref[:, pl.ds(k * 256, WIDE)]
        picked = jnp.dot(planes, weave_ref[...], preferred_element_type=f32)[:, :wide] * factor
        row = lax.broadcasted_iota(jnp.int32, (YCAP, wide), 0)
        slot = (lax.broadcasted_iota(jnp.int32, (YCAP, wide), 1) + k * 256) >> 3
        valid = (row < y_extent) & (slot < z_extent)
        vp_out_ref[:, span] = jnp.where(valid, vp_ref[:, span].astype(f32) * (1.0 + picked), 0.0)
        vs_out_ref[:, span] = jnp.where(valid, vs_ref[:, span].astype(f32) * (1.0 + picked), 0.0)
        rho_out_ref[:, span] = jnp.where(valid, rho_ref[:, span].astype(f32) * (1.0 + DENSITY_GAIN * picked), 0.0)
        pairs = ((vp_out_ref, new_vp_ref), (vs_out_ref, new_vs_ref), (rho_out_ref, new_rho_ref))
        for i, (a, b) in enumerate(pairs):
            stores.append(pltpu.make_async_copy(a.at[:, span], b.at[:, span], sem.at[i, k]))
            stores[-1].start()
    for store in stores:
        store.wait()


SMEM = pl.BlockSpec(memory_space=pltpu.SMEM)
VMEM = pl.BlockSpec(memory_space=pltpu.VMEM)
HBM = pl.BlockSpec(memory_space=pltpu.HBM)


def held(array):
    return pltpu.with_memory_space_constraint(array, pltpu.HBM)


def depth_stage(spec, wave):
    return pl.pallas_call(
        depth_kernel,
        out_shape=[pltpu.VMEM((GY, 2 * BAND, ROWS), bf16), pltpu.VMEM(wave.shape, bf16)],
        in_specs=[HBM, HBM, HBM, HBM],
        out_specs=[VMEM, VMEM],
        scratch_shapes=[
            pltpu.VMEM((2, ROWS, NZ), bf16),
            pltpu.VMEM((OUTER, ROWS, 2 * INNER), bf16),
            pltpu.VMEM((2, 2, NZ, 128), f32),
            pltpu.VMEM((2 * OUTER, INNER), f32),
            pltpu.VMEM((2 * INNER, 2 * INNER), bf16),
            pltpu.SemaphoreType.DMA((ROWS // CHUNK,)),
            pltpu.SemaphoreType.DMA((3,)),
        ],
        compiler_params=pltpu.CompilerParams(vmem_limit_bytes=32 * MIB),
    )(held(spec), held(jnp.asarray(depth_twist())), held(jnp.asarray(inner_table())), held(wave))


def y_stage(y_bounds, z_bounds, turned, taper, wave, *models):
    return pl.pallas_call(
        y_kernel,
        out_shape=[pltpu.VMEM((GY * GZ * DEEP, WIDE), bf16)] + [pltpu.VMEM(m.shape, bf16) for m in models],
        in_specs=[SMEM, SMEM, VMEM, VMEM, VMEM, VMEM, HBM, HBM, HBM],
        out_specs=[VMEM] * 4,
        scratch_shapes=[
            pltpu.VMEM((RADIX * BAND, 2 * LONG), bf16),
            pltpu.VMEM((LONG // 128, RADIX * BAND, 128), f32),
            pltpu.VMEM((MANY, TILES, BAND + DEEP, 128), f32),
            pltpu.SemaphoreType.DMA((3,)),
        ],
        compiler_params=pltpu.CompilerParams(vmem_limit_bytes=32 * MIB),
    )(y_bounds, z_bounds, turned, taper, y_twist(), wave, *[held(m) for m in models])


def model_stage(y_bounds, z_bounds, bricks, vp, vs, rho):
    flat = X * ZCAP
    whole = pltpu.VMEM((YCAP, flat), f32)
    return pl.pallas_call(
        model_kernel,
        out_shape=[jax.ShapeDtypeStruct((YCAP, flat), f32)] * 3,
        in_specs=[SMEM, SMEM, VMEM, VMEM, VMEM, VMEM],
        out_specs=[HBM] * 3,
        scratch_shapes=[
            pltpu.VMEM((YCAP, GY * X * DEEP + 128), bf16),
            pltpu.VMEM((WIDE, 256), bf16),
            whole,
            whole,
            whole,
            pltpu.SemaphoreType.DMA((3, -(-flat // 256))),
        ],
        compiler_params=pltpu.CompilerParams(vmem_limit_bytes=32 * MIB),
    )(y_bounds, z_bounds, bricks, vp, vs, rho)


def shards(spectrum, layer_index, y_bounds, z_bounds, vp, vs, rho):
    gy_index = lax.axis_index("gy")
    taper_all = (layer_index.astype(f32) + 1.0) / LAYERS
    taper_band = lax.dynamic_index_in_dim(taper_all.reshape(BAND // DEEP, GY, DEEP), gy_index, 1, False).reshape(BAND)
    taper = jnp.broadcast_to(jnp.tile(taper_band, RADIX)[:, None], (RADIX * BAND, 128))
    turned, wave = depth_stage(spectrum.reshape(2, ROWS, NZ), jnp.asarray(y_table()))
    turned = lax.all_to_all(turned, "gy", 0, 0, tiled=True)
    bricks, *models = y_stage(y_bounds, z_bounds, turned, taper, wave, vp, vs, rho)
    bricks = lax.all_to_all(bricks.reshape(GY * GZ, DEEP, WIDE), ("gy", "gz"), 0, 0, tiled=True)
    bricks = bricks.reshape(GY * X * DEEP, WIDE)
    return tuple(model_stage(y_bounds, z_bounds, bricks, *models))


def solution(mesh):
    return jax.shard_map(
        shards,
        mesh=mesh,
        in_specs=(
            P(None, "gz", "gy", None),
            P(),
            P(),
            P(),
            P("gy", "gz"),
            P("gy", "gz"),
            P("gy", "gz"),
        ),
        out_specs=(P("gy", "gz"), P("gy", "gz"), P("gy", "gz")),
        check_vma=False,
    )
```
